512 devices in a mesh: gx: 8 (over y, core), gy: 4 (over x), gz: 16 (over z).
Axes of the slice: x: 4, y: 4, z: 16, core: 2. Of those that a mesh axis runs over, the one named last changes fastest.
Arguments:
- displacement: float32 [6, 32, 32, 2048], P(None, 'gx', 'gy', 'gz'), may hold values from -6 to 6
- velocity: float32 [6, 32, 32, 2048], P(None, 'gx', 'gy', 'gz'), may hold values from -6 to 6
- moments: float32 [6, 32, 32, 2048], P(None, 'gx', 'gy', 'gz'), may hold values from -6 to 6
- sector_bit: int32 [2, 32, 32, 2048], P(None, 'gx', 'gy', 'gz'), may hold values from 0 to 1
- weight_in: bfloat16 [32, 256], replicated, may hold values from -1 to 1
- bias_in: float32 [256], replicated, may hold values from -3 to 3
- weight_mid: bfloat16 [256, 256], replicated, may hold values from -0.375 to 0.375
- weight_out: bfloat16 [256, 4], replicated, may hold values from -0.375 to 0.375
Outputs:
- displacement_out: float32 [6, 32, 32, 2048], P(None, 'gx', 'gy', 'gz')
- velocity_out: float32 [6, 32, 32, 2048], P(None, 'gx', 'gy', 'gz')
- moments_out: float32 [6, 32, 32, 2048], P(None, 'gx', 'gy', 'gz')
The draws below stay inside these ranges and needn't reach their ends.
All inputs are finite; a program needn't handle non-finite values.
Results may differ from the reference program's by a relative error of at most 0.0014.
Values sent between devices are 32-bit elements; how exact they have to be, the bound alone decides.
A program may use at most 64 MiB of HBM per device.

```python
import jax
import jax.numpy as jnp
from jax import lax

FEAT = 32
HID = 256
NX = 32
NY = 32
NZ = 2048


def touch_ends(values, rng, least, largest):
    longest = values.shape.index(max(values.shape))
    spots = []
    for shift in (0, 1):
        where = [jax.random.randint(jax.random.fold_in(rng, axis), (), 0, length) for axis, length in enumerate(values.shape)]
        where[longest] = (where[longest] + shift) % values.shape[longest]
        spots.append(tuple(where))
    return values.at[spots[0]].set(least).at[spots[1]].set(largest)


def block_levels(stream_key, extent, pieces, least, high):
    def one(dim, parts):
        steps = jax.random.uniform(jax.random.fold_in(jax.random.fold_in(stream_key, 6), dim), (parts,), jnp.float32, least / len(pieces), high / len(pieces))
        return jnp.repeat(jnp.exp(steps), extent[dim] // parts).reshape((-1,) + (1,) * (len(extent) - dim - 1))

    level = one(*pieces[0])
    for cut in pieces[1:]:
        level = level * one(*cut)
    return level


def centred(stream_key, extent, deviation, reach, shards=(), held_as=jnp.bfloat16):
    entries = jax.random.normal(stream_key, extent, jnp.float32) * deviation
    if len(shards) > 0:
        entries = block_levels(stream_key, extent, shards, -0.22, 0.18) * entries
    return jnp.clip(entries, min=-reach, max=reach).astype(held_as)


def setup_inputs(seed: int = 0) -> dict:
    splits = jax.random.split(jax.random.key(seed), 9)
    displacement = centred(splits[0], (6, NX, NY, NZ), 1.0, 6.0, ((1, 8), (2, 4), (3, 16)), jnp.float32)
    velocity = centred(splits[1], (6, NX, NY, NZ), 1.0, 6.0, ((1, 8), (2, 4), (3, 16)), jnp.float32)
    moments = centred(splits[2], (6, NX, NY, NZ), 1.0, 6.0, ((1, 8), (2, 4), (3, 16)), jnp.float32)
    sector_bit = touch_ends(jax.random.randint(splits[3], (2, NX, NY, NZ), 0, 2), jax.random.fold_in(splits[3], 1), 0, 1).astype(jnp.int32)
    weight_in = centred(splits[4], (FEAT, HID), FEAT ** -0.5, 1.0)
    bias_in = centred(splits[5], (HID,), 0.5, 3.0, (), jnp.float32)
    weight_mid = centred(splits[6], (HID, HID), HID ** -0.5, 0.375)
    weight_out = centred(splits[7], (HID, 4), HID ** -0.5, 0.375)
    return {"displacement": displacement, "velocity": velocity, "moments": moments, "sector_bit": sector_bit, "weight_in": weight_in, "bias_in": bias_in, "weight_mid": weight_mid, "weight_out": weight_out}


half_step = 0.1
lattice_step = 0.25
second_shell = 0.5

def offsets(part):
    sign = 2 * part - 1
    return [(sign * (corner >> 2 & 1), sign * (corner >> 1 & 1), sign * (corner & 1)) for corner in range(8)]

def shifted(field, offset):
    return jnp.roll(field, (-offset[0], -offset[1], -offset[2]), (1, 2, 3))

def features(displacement, moments, part):
    other = 1 - part
    own_disp = displacement[3 * part:3 * part + 3]
    own_spin = moments[3 * part:3 * part + 3]
    rows = []
    for offset in offsets(part):
        near_disp = shifted(displacement[3 * other:3 * other + 3], offset)
        near_spin = shifted(moments[3 * other:3 * other + 3], offset)
        rows.append(near_disp - own_disp)
        rows.append(lax.optimization_barrier(jnp.sum(own_spin * near_spin, axis=0, keepdims=True)))
    return jnp.concatenate(rows, 0).astype(jnp.bfloat16)

def network(block, weight_in, bias_in, weight_mid, weight_out):
    dims = (((0,), (0,)), ((), ()))
    first = lax.dot_general(weight_in, block, dims, preferred_element_type=jnp.float32)
    first = jax.nn.silu(first + bias_in[:, None]).astype(jnp.bfloat16)
    second = lax.dot_general(weight_mid, first, dims, preferred_element_type=jnp.float32)
    second = jax.nn.silu(second).astype(jnp.bfloat16)
    return lax.dot_general(weight_out, second, dims, preferred_element_type=jnp.float32)

def heads_of(table, weight_in, bias_in, weight_mid, weight_out):
    width, size_x, size_y, size_z = table.shape
    blocks = table.reshape(width, size_x * size_y, size_z).transpose(1, 0, 2)
    result = lax.map(lambda block: network(block, weight_in, bias_in, weight_mid, weight_out), blocks)
    return result.transpose(1, 0, 2).reshape(4, size_x, size_y, size_z)

def rotate(moment, field, step):
    square = lax.optimization_barrier(jnp.sum(field * field, axis=0))
    theta = step * jnp.sqrt(square)
    along = jnp.sinc(theta / jnp.pi)
    across = 0.5 * jnp.sinc(theta / (2.0 * jnp.pi)) ** 2
    cross = jnp.stack([field[1] * moment[2] - field[2] * moment[1], field[2] * moment[0] - field[0] * moment[2], field[0] * moment[1] - field[1] * moment[0]])
    inner = lax.optimization_barrier(jnp.sum(field * moment, axis=0))
    return jnp.cos(theta) * moment + step * along * cross + step * step * across * inner * field

def reference(displacement, velocity, moments, sector_bit, weight_in, bias_in, weight_mid, weight_out):
    size_x, size_y, size_z = (displacement.shape[1], displacement.shape[2], displacement.shape[3])
    heads_zero = heads_of(features(displacement, moments, 0), weight_in, bias_in, weight_mid, weight_out)
    heads_one = heads_of(features(displacement, moments, 1), weight_in, bias_in, weight_mid, weight_out)
    force = jnp.concatenate([heads_zero[0:3], heads_one[0:3]], 0)
    coupling = 1.0 + 0.5 * jnp.tanh(jnp.stack([heads_zero[3], heads_one[3]]))
    velocity_out = velocity + lattice_step * force
    displacement_out = displacement + lattice_step * velocity_out
    grid = (size_x, size_y, size_z)
    index_x = lax.broadcasted_iota(jnp.int32, grid, 0)
    index_y = lax.broadcasted_iota(jnp.int32, grid, 1)
    index_z = lax.broadcasted_iota(jnp.int32, grid, 2)
    parity = (index_x + index_y + index_z) % 2
    sector_map = 4 * jnp.arange(2, dtype=jnp.int32)[:, None, None, None] + 2 * sector_bit + parity[None]
    spins = moments
    for sector in list(range(8)) + list(range(7, -1, -1)):
        part = sector // 4
        other = 1 - part
        own = spins[3 * part:3 * part + 3]
        near = spins[3 * other:3 * other + 3]
        near_total = jnp.zeros(own.shape, jnp.float32)
        for offset in offsets(part):
            near_total = near_total + shifted(near, offset)
        shell = jnp.zeros(own.shape, jnp.float32)
        for axis_offset in ((1, 0, 0), (-1, 0, 0), (0, 1, 0), (0, -1, 0), (0, 0, 1), (0, 0, -1)):
            shell = shell + shifted(own, axis_offset)
        field = coupling[part][None] * near_total + second_shell * shell
        turned = rotate(own, field, half_step)
        updated = jnp.where((sector_map[part] == sector)[None], turned, own)
        if part == 0:
            spins = jnp.concatenate([updated, near], 0)
        else:
            spins = jnp.concatenate([near, updated], 0)
    return (displacement_out, velocity_out, spins)
```

```python
import functools
import itertools

import jax
import jax.numpy as jnp
from jax import lax
from jax.experimental import pallas as pl
from jax.experimental.pallas import tpu as pltpu
from jax.sharding import PartitionSpec as P

AXES = ("gx", "gy", "gz")
MESH = pl.DeviceIdType.MESH
F32 = jnp.float32
BF16 = jnp.bfloat16

DIRS = sorted(
    (d for d in itertools.product((-1, 0, 1), repeat=3) if d != (0, 0, 0)),
    key=lambda d: -sum(abs(c) for c in d),
)
UP = [d for d in DIRS if min(d) >= 0]
DOWN = [d for d in DIRS if max(d) <= 0]
GROUPS = {"d1": 3, "m1": 3, "d0": 3, "m0": 3, "c0": 2, "c1": 2, "e1": 3, "e2": 3, "e3": 3}
NAMES = list(GROUPS)


def kernel(
    disp, vel, mom, bits, w_in, bias, w_mid, w_out,
    disp_out, vel_out, mom_out,
    *scratch,
):
    n = len(NAMES)
    flat = dict(zip(NAMES, scratch[:n]))
    edge = dict(zip(NAMES, scratch[n : 2 * n]))
    strip, landed, drive, table, heads, w1, w2, w3, bias_wide, send_sem, recv_sem = scratch[2 * n :]

    size = [lax.axis_size(a) for a in AXES]
    me = [lax.axis_index(a) for a in AXES]
    beside = [
        {-1: lax.rem(i + s - 1, s), 0: i, 1: lax.rem(i + 1, s)} for i, s in zip(me, size)
    ]

    def device(d):
        return tuple(beside[k][d[k]] for k in range(3))

    barrier = pltpu.get_barrier_semaphore()
    for d in DIRS:
        pl.semaphore_signal(barrier, inc=1, device_id=device(d), device_id_type=MESH)

    row = lax.broadcasted_iota(jnp.int32, (8, 128), 0)
    lane = lax.broadcasted_iota(jnp.int32, (8, 128), 1)
    odd = (row + lane) % 2 == 1
    behind = lane % 8 >= 4
    first_lane, last_lane = lane == 0, lane == 127
    first_row, last_row = row == 0, row == 7

    def by_parity(even_plane, odd_plane):
        return jnp.where(odd, odd_plane, even_plane), jnp.where(odd, even_plane, odd_plane)

    def pack(name):
        ref = flat[name]
        total = jnp.zeros((8, 128), F32)
        j = 0
        for f in range(GROUPS[name]):
            for par in range(2):
                for i in range(2):
                    turned = ref[f, par, 2 + i, 0]
                    if j:
                        turned = pltpu.roll(turned, 8 * j, 1)
                    total = jnp.where((lane + 4) // 8 % 16 == j, turned, total)
                    j += 1
        strip[NAMES.index(name)] = total

    def copy(name, d):
        g, k = NAMES.index(name), DIRS.index(d)
        rows = {0: slice(0, 8), 1: slice(4, 8), -1: slice(0, 4)}[d[1]]
        side, tile = 1 - d[0], abs(d[1])
        if d[2]:
            src = strip.at[g, rows]
            dst = landed.at[g, side, tile, (d[2] + 1) // 2, rows]
        else:
            src = flat[name].at[:, :, 2:4, 0, rows]
            dst = flat[name].at[:, :, 2 * side : 2 * side + 2, tile, rows]
        return pltpu.make_async_remote_copy(
            src_ref=src, dst_ref=dst, send_sem=send_sem.at[g, k], recv_sem=recv_sem.at[g, k],
            device_id=device(d), device_id_type=MESH,
        )

    def send(name, dirs):
        for d in dirs:
            copy(name, d).start()

    def arrive(name, dirs):
        for d in dirs:
            copy(name, d).wait_recv()

    def sent(name, dirs=DIRS):
        for d in dirs:
            copy(name, d).wait_send()

    def unpack(name, sides=(0, 1, 2)):
        g = NAMES.index(name)
        for side in sides:
            for tile in range(2):
                both = jnp.where(behind, landed[g, side, tile, 1], landed[g, side, tile, 0])
                j = 0
                for f in range(GROUPS[name]):
                    for par in range(2):
                        for i in range(2):
                            turned = pltpu.roll(both, (128 - 8 * j) % 128, 1) if j else both
                            edge[name][f, par, 2 * side + i, tile] = turned
                            j += 1

    def load_own(name, source, first, count):
        for f in range(count):
            for i in range(2):
                pair = by_parity(source[first + f, 2 * i], source[first + f, 2 * i + 1])
                flat[name][f, 0, 2 + i, 0] = pair[0]
                flat[name][f, 1, 2 + i, 0] = pair[1]
        pack(name)

    load_own("d1", disp, 3, 3)
    load_own("m1", mom, 3, 3)
    load_own("d0", disp, 0, 3)
    load_own("m0", mom, 0, 3)
    pl.semaphore_wait(barrier, len(DIRS))
    send("m1", DIRS)
    send("d1", UP)
    send("m0", DIRS)
    send("d0", DOWN)

    w1[...] = (w_in[...].astype(F32).T * 0.5).astype(BF16)
    w2[...] = (w_mid[...].astype(F32).T * 0.5).astype(BF16)
    w3[...] = jnp.concatenate([w_out[...].astype(F32).T, jnp.zeros((12, 256), F32)], 0).astype(BF16)
    bias_wide[...] = jnp.broadcast_to(bias[...].reshape(1, 256) * 0.5, (128, 256)).T

    def shift_z(near, far, sign):
        by, last = (127, last_lane) if sign > 0 else (1, first_lane)
        axis = near.ndim - 1
        return jnp.where(last, pltpu.roll(far, by, axis), pltpu.roll(near, by, axis))

    def shift_y(near, far, sign):
        by, last = (7, last_row) if sign > 0 else (1, first_row)
        axis = near.ndim - 2
        return jnp.where(last, pltpu.roll(far, by, axis), pltpu.roll(near, by, axis))

    def odd_of(par):
        return odd if par == 0 else jnp.logical_not(odd)

    def beside_x(ref, par, i, sign):
        far = min(max(i + sign, 0), 5)
        here, there = ref[:, 1 - par, i], ref[:, 1 - par, far]
        crosses = odd_of(par) if sign > 0 else odd_of(1 - par)
        return jnp.where(crosses, there, here)

    def features(p):
        q, sign = 1 - p, 2 * p - 1
        for i in range(2):
            pair = 2 + i
            cells = {}
            for kind in ("d", "m"):
                name = kind + str(q)
                for dx in range(2):
                    for par in range(2):
                        if dx:
                            near = beside_x(flat[name], par, pair, sign)
                            far = beside_x(edge[name], par, pair, sign)
                        else:
                            near, far = flat[name][:, par, pair], edge[name][:, par, pair]
                        cells[kind, dx, par, 0] = near
                        cells[kind, dx, 1 - par, 1] = shift_z(near, far, sign)
            for par in range(2):
                own_d = flat["d" + str(p)][:, par, pair, 0]
                own_m = flat["m" + str(p)][:, par, pair, 0]
                at = (par * 2 + i) * 8
                for o in range(8):
                    dx, dy, dz = o // 4, o // 2 % 2, o % 2
                    held = (par + dy) % 2
                    near_d, near_m = cells["d", dx, held, dz], cells["m", dx, held, dz]
                    if dy:
                        near_d = shift_y(near_d[:, 0], near_d[:, 1], sign)
                        near_m = shift_y(near_m[:, 0], near_m[:, 1], sign)
                    else:
                        near_d, near_m = near_d[:, 0], near_m[:, 0]
                    diff = near_d - own_d
                    for k in range(3):
                        table[pl.ds((4 * o + k) * 32 + at, 8), :] = diff[k]
                    table[pl.ds((4 * o + 3) * 32 + at, 8), :] = jnp.sum(own_m * near_m, axis=0)

    def network(p):
        @pl.loop(0, 8)
        def _(chunk):
            x = jnp.concatenate(
                [table[pl.ds(chunk * 4 + r, 32, stride=32), :] for r in range(4)], axis=1
            ).astype(BF16)
            wide = jnp.concatenate([bias_wide[...]] * 4, axis=1)
            h = jnp.dot(w1[...], x, preferred_element_type=F32) + wide
            h = (h + h * jnp.tanh(h)).astype(BF16)
            h = jnp.dot(w2[...], h, preferred_element_type=F32)
            h = (h + h * jnp.tanh(h)).astype(BF16)
            h = jnp.dot(w3[...], h, preferred_element_type=F32)
            for r in range(4):
                heads[pl.ds((chunk * 4 + r) * 8, 8), :] = h[0:8, 128 * r : 128 * r + 128]

        def head(k, par, i):
            return heads[pl.ds((par * 2 + i) * 64 + k, 8, stride=8), :]

        name = "c" + str(p)
        for i in range(2):
            for k in range(3):
                planes = by_parity(head(k, 0, i), head(k, 1, i))
                for x in range(2):
                    v = vel[3 * p + k, 2 * i + x] + 0.25 * planes[x]
                    vel_out[3 * p + k, 2 * i + x] = v
                    disp_out[3 * p + k, 2 * i + x] = disp[3 * p + k, 2 * i + x] + 0.25 * v
            for par in range(2):
                flat[name][0, par, 2 + i, 0] = 1.0 + 0.5 * jnp.tanh(head(3, par, i))
            pair = by_parity(bits[p, 2 * i].astype(F32), bits[p, 2 * i + 1].astype(F32))
            for par in range(2):
                flat[name][1, par, 2 + i, 0] = pair[par]
        pack(name)
        send(name, DIRS)

    arrive("m1", DIRS)
    arrive("d1", UP)
    unpack("m1")
    unpack("d1", (0, 1))
    features(0)
    network(0)
    arrive("m0", DIRS)
    arrive("d0", DOWN)
    unpack("m0")
    unpack("d0", (1, 2))
    features(1)
    network(1)

    def drives(p, source):
        q, sign = 1 - p, 2 * p - 1
        name = "c" + str(p)

        def body(i):
            for k in range(3):
                along = []
                for par in range(2):
                    along.append([])
                    for ref in (flat[source], edge[source]):
                        far = min(max(i + sign, 0), 5)
                        crosses = odd_of(par) if sign > 0 else odd_of(1 - par)
                        other = jnp.where(crosses, ref[k, 1 - par, far], ref[k, 1 - par, i])
                        along[par].append(ref[k, par, i] + other)
                tall = []
                for par in range(2):
                    tall.append([])
                    for z in range(2):
                        o = along[1 - par][z]
                        s = shift_y(o, jnp.stack([o[1], o[0]]), sign)
                        tall[par].append(along[par][z] + s)
                for par in range(2):
                    near = tall[par][0] + shift_z(tall[1 - par][0], tall[1 - par][1], sign)
                    far_ = tall[par][1] + shift_z(tall[1 - par][1], tall[1 - par][0], sign)
                    drive[0, k, par, i] = near * flat[name][0, par, i]
                    drive[1, k, par, i] = far_ * edge[name][0, par, i]

        for i in range(6):
            body(i)

    def turn(v, b, twice):
        square = b[0] * b[0] + b[1] * b[1] + b[2] * b[2]
        z = square * (0.0025 / 64.0)
        c = 1.0 + z * (-1 / 2 + z * (1 / 24 + z * (-1 / 720 + z * (1 / 40320 - z / 3628800))))
        s = 0.05 + z * (-0.05 / 6 + z * (0.05 / 120 + z * (-0.05 / 5040 + z * (0.05 / 362880))))
        for _ in range(3):
            s = s * c
            c = 2.0 * (c * c) - 1.0
        if twice:
            s = 2.0 * (s * c)
            c = 2.0 * (c * c) - 1.0
        q = [s * b[k] for k in range(3)]
        w = [v[k] + v[k] for k in range(3)]
        t = [q[1] * w[2] - q[2] * w[1], q[2] * w[0] - q[0] * w[2], q[0] * w[1] - q[1] * w[0]]
        r = [q[1] * t[2] - q[2] * t[1], q[2] * t[0] - q[0] * t[2], q[0] * t[1] - q[1] * t[0]]
        return [v[k] + (c * t[k] + r[k]) for k in range(3)]

    def step(p, name, sector, extent, twice=False):
        par, bit = sector % 2, float(sector // 2 % 2)
        lo, hi = {3: (0, 6), 2: (1, 5), 1: (1, 5), 0: (2, 4)}[extent]
        refs = (flat[name], edge[name])
        opened = odd_of(par)
        fields = (flat["c" + str(p)], edge["c" + str(p)])
        for i in range(lo, hi):
            inner = [[ref[k, 1 - par, i] for ref in refs] for k in range(3)]
            field = []
            for k in range(3):
                field.append([])
                for z in range(1 if extent == 0 else 2):
                    o, far = inner[k][z], inner[k][1 - z]
                    back = refs[z][k, 1 - par, max(i - 1, 0)]
                    ahead = refs[z][k, 1 - par, min(i + 1, 5)]
                    flipped = jnp.stack([o[1], o[0]])
                    total = o + jnp.where(opened, ahead, back)
                    total = total + shift_y(o, flipped, 1) + shift_y(o, flipped, -1)
                    total = total + shift_z(o, far, 1) + shift_z(o, far, -1)
                    field[k].append(0.5 * total + drive[z, k, par, i])
            for z in range(1 if extent == 0 else 2):
                own = [refs[z][k, par, i] for k in range(3)]
                b = [field[k][z] for k in range(3)]
                chosen = fields[z][1, par, i] == bit
                if extent == 0:
                    own, b, chosen = [v[0] for v in own], [v[0] for v in b], chosen[0]
                new = turn(own, b, twice)
                for k in range(3):
                    value = jnp.where(chosen, new[k], own[k])
                    if extent == 0:
                        refs[z][k, par, i, 0] = value
                    else:
                        refs[z][k, par, i] = value

    def own_to(name, source):
        flat[name][:, :, 2:4, 0] = flat[source][:, :, 2:4, 0]
        pack(name)
        send(name, DIRS)

    arrive("c0", DIRS)
    unpack("c0")
    drives(0, "m1")
    sent("m0")
    for k, sector in enumerate((0, 1, 2, 3)):
        step(0, "m0", sector, 3 - k)
    own_to("e1", "m0")
    arrive("c1", DIRS)
    unpack("c1")
    arrive("e1", DIRS)
    unpack("e1")
    drives(1, "e1")
    sent("m1")
    for k, sector in enumerate((4, 5, 6, 7)):
        step(1, "m1", sector, 3 - k, sector == 7)
    own_to("e2", "m1")
    arrive("e2", DIRS)
    unpack("e2")
    sent("e2")
    for k, sector in enumerate((6, 5, 4)):
        step(1, "e2", sector, 2 - k)
    own_to("e3", "e2")
    arrive("e3", DIRS)
    unpack("e3")
    drives(0, "e3")
    sent("e1")
    for k, sector in enumerate((3, 2, 1, 0)):
        step(0, "e1", sector, 3 - k)
    for p, name in ((0, "e1"), (1, "e2")):
        for k in range(3):
            for i in range(2):
                planes = by_parity(flat[name][k, 0, 2 + i, 0], flat[name][k, 1, 2 + i, 0])
                for x in range(2):
                    mom_out[3 * p + k, 2 * i + x] = planes[x]

    sent("d1", UP)
    sent("d0", DOWN)
    for name in ("c0", "c1", "e3"):
        sent(name)


def on_device(displacement, velocity, moments, sector_bit, weight_in, bias_in, weight_mid, weight_out):
    vmem = pl.BlockSpec(memory_space=pltpu.VMEM)
    shape = jax.ShapeDtypeStruct(displacement.shape, F32)
    count = len(NAMES)
    groups = [pltpu.VMEM((f, 2, 6, 2, 8, 128), F32) for f in GROUPS.values()]
    return pl.pallas_call(
        kernel,
        out_shape=(shape, shape, shape),
        in_specs=[vmem] * 8,
        out_specs=(vmem, vmem, vmem),
        scratch_shapes=groups
        + groups
        + [
            pltpu.VMEM((count, 8, 128), F32),
            pltpu.VMEM((count, 3, 2, 2, 8, 128), F32),
            pltpu.VMEM((2, 3, 2, 6, 2, 8, 128), F32),
            pltpu.VMEM((1024, 128), F32),
            pltpu.VMEM((256, 128), F32),
            pltpu.VMEM((256, 32), BF16),
            pltpu.VMEM((256, 256), BF16),
            pltpu.VMEM((16, 256), BF16),
            pltpu.VMEM((256, 128), F32),
            pltpu.SemaphoreType.DMA((count, len(DIRS))),
            pltpu.SemaphoreType.DMA((count, len(DIRS))),
        ],
        compiler_params=pltpu.CompilerParams(
            collective_id=0, has_side_effects=True, vmem_limit_bytes=40 * 1024 * 1024
        ),
    )(displacement, velocity, moments, sector_bit, weight_in, bias_in, weight_mid, weight_out)


def solution(mesh):
    cells = P(None, "gx", "gy", "gz")
    return jax.shard_map(
        on_device,
        mesh=mesh,
        in_specs=(cells, cells, cells, cells, P(), P(), P(), P()),
        out_specs=(cells, cells, cells),
        check_vma=False,
    )
```

```python
import functools
import itertools

import jax
import jax.numpy as jnp
from jax import lax
from jax.experimental import pallas as pl
from jax.experimental.pallas import tpu as pltpu
from jax.sharding import PartitionSpec as P

AXES = ("gx", "gy", "gz")
MESH = pl.DeviceIdType.MESH
F32 = jnp.float32
BF16 = jnp.bfloat16

DIRS = sorted(
    (d for d in itertools.product((-1, 0, 1), repeat=3) if d != (0, 0, 0)),
    key=lambda d: -sum(abs(c) for c in d),
)
UP = [d for d in DIRS if min(d) >= 0]
DOWN = [d for d in DIRS if max(d) <= 0]
GROUPS = {"f1": 6, "f0": 6, "m1": 3, "m0": 3, "c0": 2, "c1": 2, "e1": 3, "e2": 3, "e3": 3}
NAMES = list(GROUPS)


def kernel(
    disp_in, vel_in, mom_in, bits_in, w_in_in, bias_in, w_mid_in, w_out_in,
    disp_out, vel_out, mom_out,
    *scratch,
):
    n = len(NAMES)
    flat = dict(zip(NAMES, scratch[:n]))
    edge = dict(zip(NAMES, scratch[n : 2 * n]))
    strip, landed, strip_f, landed_f, drive, table, heads, w1, w2, w3, bias_wide = scratch[2 * n : 2 * n + 11]
    disp, vel, mom, bits, w_in, bias, w_mid, w_out, in_sem, send_sem, recv_sem, send_sem_f, recv_sem_f = scratch[2 * n + 11 :]
    given = (
        (mom_in, mom), (disp_in, disp), (w_in_in, w_in), (bias_in, bias), (w_mid_in, w_mid),
        (w_out_in, w_out), (vel_in, vel), (bits_in, bits),
    )
    loads = [pltpu.make_async_copy(a, b, in_sem.at[k]) for k, (a, b) in enumerate(given)]
    for load in loads:
        load.start()

    size = [lax.axis_size(a) for a in AXES]
    me = [lax.axis_index(a) for a in AXES]
    beside = [
        {-1: lax.rem(i + s - 1, s), 0: i, 1: lax.rem(i + 1, s)} for i, s in zip(me, size)
    ]

    def device(d):
        return tuple(beside[k][d[k]] for k in range(3))

    barrier = pltpu.get_barrier_semaphore()
    for d in DIRS:
        pl.semaphore_signal(barrier, inc=1, device_id=device(d), device_id_type=MESH)

    row = lax.broadcasted_iota(jnp.int32, (8, 128), 0)
    lane = lax.broadcasted_iota(jnp.int32, (8, 128), 1)
    odd = (row + lane) % 2 == 1
    behind = lane % 8 >= 4
    first_lane, last_lane = lane == 0, lane == 127
    first_row, last_row = row == 0, row == 7

    def by_parity(even_plane, odd_plane):
        return jnp.where(odd, odd_plane, even_plane), jnp.where(odd, even_plane, odd_plane)

    def pack(ref, first, fields):
        total = jnp.zeros((8, 128), F32)
        j = 0
        for f in range(fields):
            for par in range(2):
                for i in range(2):
                    turned = ref[first + f, par, 2 + i, 0]
                    if j:
                        turned = pltpu.roll(turned, 8 * j, 1)
                    total = jnp.where((lane + 4) // 8 % 16 == j, turned, total)
                    j += 1
        return total

    def send(name, source, first=0):
        g, fields = NAMES.index(name), GROUPS[name]
        strip[g] = pack(source, first, fields)
        for d in DIRS:
            rows = {0: slice(0, 8), 1: slice(4, 8), -1: slice(0, 4)}[d[1]]
            side, tile = 1 - d[0], abs(d[1])
            if d[2]:
                src = strip.at[g, rows]
                dst = landed.at[g, side, tile, (d[2] + 1) // 2, rows]
            else:
                src = source.at[first : first + fields, :, 2:4, 0, rows]
                dst = flat[name].at[:, :, 2 * side : 2 * side + 2, tile, rows]
            k = abs(d[2])
            pltpu.make_async_remote_copy(
                src_ref=src, dst_ref=dst, send_sem=send_sem.at[g, k], recv_sem=recv_sem.at[g, k],
                device_id=device(d), device_id_type=MESH,
            ).start()

    def both_waits(name, sems):
        g = NAMES.index(name)
        cells, strips = flat[name].at[:, :, 0:5], landed.at[g]
        pltpu.make_async_copy(cells, cells, sems.at[g, 0]).wait()
        pltpu.make_async_copy(strips, strips, sems.at[g, 1]).wait()

    def arrive(name):
        both_waits(name, recv_sem)
        unpack(name)

    def sent(name):
        both_waits(name, send_sem)

    def unpack(name):
        g = NAMES.index(name)
        for side in range(3):
            for tile in range(2):
                both = jnp.where(behind, landed[g, side, tile, 1], landed[g, side, tile, 0])
                j = 0
                for f in range(GROUPS[name]):
                    for par in range(2):
                        for i in range(2):
                            turned = pltpu.roll(both, 128 - 8 * j, 1) if j else both
                            edge[name][f, par, 2 * side + i, tile] = turned
                            j += 1

    def copies_f(p):
        ref = flat["f" + str(p)]
        for k, d in enumerate(UP if p else DOWN):
            rows = {0: slice(0, 8), 1: slice(4, 8), -1: slice(0, 4)}[d[1]]
            side, tile = 1 - d[0], abs(d[1])
            if d[2]:
                src, dst = strip_f.at[p, :, rows], landed_f.at[p, side, tile, :, rows]
            else:
                here = {0: slice(2, 4), 1: slice(3, 4), -1: slice(2, 3)}[d[0]]
                there = {0: slice(2, 4), 1: slice(1, 2), -1: slice(4, 5)}[d[0]]
                src, dst = ref.at[:, :, here, 0, rows], ref.at[:, :, there, tile, rows]
            yield pltpu.make_async_remote_copy(
                src_ref=src, dst_ref=dst, send_sem=send_sem_f.at[p, k], recv_sem=recv_sem_f.at[p, k],
                device_id=device(d), device_id_type=MESH,
            )

    def arrive_f(p):
        for c in copies_f(p):
            c.wait_recv()
        for side in (0, 1) if p else (1, 2):
            for tile in range(2):
                for kind in range(2):
                    got = landed_f[p, side, tile, kind]
                    j = 0
                    for f in range(3):
                        for par in range(2):
                            for i in range(2):
                                turned = pltpu.roll(got, 128 - 8 * j, 1) if j else got
                                edge["f" + str(p)][3 * kind + f, par, 2 * side + i, tile] = turned
                                j += 1

    def load_own(p):
        ref = flat["f" + str(p)]
        for kind, source in enumerate((disp, mom)):
            for f in range(3):
                for i in range(2):
                    pair = by_parity(source[3 * p + f, 2 * i], source[3 * p + f, 2 * i + 1])
                    ref[3 * kind + f, 0, 2 + i, 0] = pair[0]
                    ref[3 * kind + f, 1, 2 + i, 0] = pair[1]
            strip_f[p, kind] = pack(ref, 3 * kind, 3)

    loads[0].wait()
    loads[1].wait()
    load_own(1)
    pl.semaphore_wait(barrier, len(DIRS))
    for c in copies_f(1):
        c.start()
    load_own(0)
    for c in copies_f(0):
        c.start()
    for p in (1, 0):
        send("m" + str(p), flat["f" + str(p)], 3)
    for load in loads[2:]:
        load.wait()
    for p in range(2):
        flat["m" + str(p)][:, :, 2:4, 0] = flat["f" + str(p)][3:6, :, 2:4, 0]

    w1[...] = (w_in[...].astype(F32).T * 0.5).astype(BF16)
    w2[...] = (w_mid[...].astype(F32).T * 0.5).astype(BF16)
    w3[...] = jnp.concatenate([w_out[...].astype(F32), jnp.zeros((12, 256), F32)], 0).astype(BF16)
    bias_wide[...] = jnp.broadcast_to(bias[...].reshape(1, 256) * 0.5, (128, 256)).T

    def shift_z(near, far, sign):
        by, last = (127, last_lane) if sign > 0 else (1, first_lane)
        axis = near.ndim - 1
        return jnp.where(last, pltpu.roll(far, by, axis), pltpu.roll(near, by, axis))

    def shift_y(near, far, sign):
        by, last = (7, last_row) if sign > 0 else (1, first_row)
        axis = near.ndim - 2
        return jnp.where(last, pltpu.roll(far, by, axis), pltpu.roll(near, by, axis))

    def odd_of(par):
        return odd if par == 0 else jnp.logical_not(odd)

    def beside_x(ref, fields, par, i, sign):
        far = min(max(i + sign, 0), 5)
        here, there = ref[fields, 1 - par, i], ref[fields, 1 - par, far]
        crosses = odd_of(par) if sign > 0 else odd_of(1 - par)
        return jnp.where(crosses, there, here)

    def features(p):
        name, sign = "f" + str(1 - p), 2 * p - 1
        for i in range(2):
            pair = 2 + i
            cells = {}
            for kind in ("d", "m"):
                fields = slice(0, 3) if kind == "d" else slice(3, 6)
                for dx in range(2):
                    for par in range(2):
                        if dx:
                            near = beside_x(flat[name], fields, par, pair, sign)
                            far = beside_x(edge[name], fields, par, pair, sign)
                        else:
                            near, far = flat[name][fields, par, pair], edge[name][fields, par, pair]
                        cells[kind, dx, par, 0] = near
                        cells[kind, dx, 1 - par, 1] = shift_z(near, far, sign)
            for par in range(2):
                own_d = flat["f" + str(p)][0:3, par, pair, 0]
                own_m = flat["f" + str(p)][3:6, par, pair, 0]
                at = (par * 2 + i) * 8
                for o in range(8):
                    dx, dy, dz = o // 4, o // 2 % 2, o % 2
                    held = (par + dy) % 2
                    near_d, near_m = cells["d", dx, held, dz], cells["m", dx, held, dz]
                    if dy:
                        near_d = shift_y(near_d[:, 0], near_d[:, 1], sign)
                        near_m = shift_y(near_m[:, 0], near_m[:, 1], sign)
                    else:
                        near_d, near_m = near_d[:, 0], near_m[:, 0]
                    diff = near_d - own_d
                    for k in range(3):
                        table[pl.ds((4 * o + k) * 32 + at, 8), :] = diff[k]
                    table[pl.ds((4 * o + 3) * 32 + at, 8), :] = jnp.sum(own_m * near_m, axis=0)

    def network(p):
        @pl.loop(0, 8)
        def _(chunk):
            x = jnp.concatenate(
                [table[pl.ds(chunk * 4 + r, 32, stride=32), :] for r in range(4)], axis=1
            ).astype(BF16)
            wide = jnp.concatenate([bias_wide[...]] * 4, axis=1)
            h = jnp.dot(w1[...], x, preferred_element_type=F32) + wide
            h = (h + h * jnp.tanh(h)).astype(BF16)
            h = jnp.dot(w2[...], h, preferred_element_type=F32)
            h = (h + h * jnp.tanh(h)).astype(BF16)
            h = jnp.dot(w3[...], h, preferred_element_type=F32)
            for r in range(4):
                heads[pl.ds((chunk * 4 + r) * 8, 8), :] = h[0:8, 128 * r : 128 * r + 128]

        def head(k, par, i):
            return heads[pl.ds((par * 2 + i) * 64 + k, 8, stride=8), :]

        name = "c" + str(p)
        for i in range(2):
            for k in range(3):
                planes = by_parity(head(k, 0, i), head(k, 1, i))
                for x in range(2):
                    v = vel[3 * p + k, 2 * i + x] + 0.25 * planes[x]
                    vel_out[3 * p + k, 2 * i + x] = v
                    disp_out[3 * p + k, 2 * i + x] = disp[3 * p + k, 2 * i + x] + 0.25 * v
            for par in range(2):
                flat[name][0, par, 2 + i, 0] = 1.0 + 0.5 * jnp.tanh(head(3, par, i))
            pair = by_parity(bits[p, 2 * i].astype(F32), bits[p, 2 * i + 1].astype(F32))
            for par in range(2):
                flat[name][1, par, 2 + i, 0] = pair[par]
        send(name, flat[name])

    arrive_f(1)
    features(0)
    network(0)
    arrive_f(0)
    features(1)
    network(1)

    def drives(p, source):
        sign = 2 * p - 1

        def body(i):
            for k in range(3):
                along = []
                for par in range(2):
                    along.append([])
                    for ref in (flat[source], edge[source]):
                        far = min(max(i + sign, 0), 5)
                        crosses = odd_of(par) if sign > 0 else odd_of(1 - par)
                        other = jnp.where(crosses, ref[k, 1 - par, far], ref[k, 1 - par, i])
                        along[par].append(ref[k, par, i] + other)
                tall = []
                for par in range(2):
                    tall.append([])
                    for z in range(2):
                        o = along[1 - par][z]
                        s = shift_y(o, jnp.stack([o[1], o[0]]), sign)
                        tall[par].append(along[par][z] + s)
                for par in range(2):
                    near = tall[par][0] + shift_z(tall[1 - par][0], tall[1 - par][1], sign)
                    beyond = tall[par][1] + shift_z(tall[1 - par][1], tall[1 - par][0], sign)
                    drive[0, k, par, i] = near
                    drive[1, k, par, i] = beyond

        for i in range(6):
            body(i)

    def turn(v, b, twice):
        square = b[0] * b[0] + b[1] * b[1] + b[2] * b[2]
        z = square * (0.0025 / 64.0)
        c = 1.0 + z * (-1 / 2 + z * (1 / 24 + z * (-1 / 720 + z * (1 / 40320 - z / 3628800))))
        s = 0.05 + z * (-0.05 / 6 + z * (0.05 / 120 + z * (-0.05 / 5040 + z * (0.05 / 362880))))
        for _ in range(3):
            s = s * c
            c = 2.0 * (c * c) - 1.0
        if twice:
            s = 2.0 * (s * c)
            c = 2.0 * (c * c) - 1.0
        q = [s * b[k] for k in range(3)]
        w = [v[k] + v[k] for k in range(3)]
        t = [q[1] * w[2] - q[2] * w[1], q[2] * w[0] - q[0] * w[2], q[0] * w[1] - q[1] * w[0]]
        r = [q[1] * t[2] - q[2] * t[1], q[2] * t[0] - q[0] * t[2], q[0] * t[1] - q[1] * t[0]]
        return [v[k] + (c * t[k] + r[k]) for k in range(3)]

    def step(p, name, sector, extent, twice=False):
        par, bit = sector % 2, float(sector // 2 % 2)
        lo, hi = {3: (0, 6), 2: (1, 5), 1: (1, 5), 0: (2, 4)}[extent]
        refs = (flat[name], edge[name])
        opened = odd_of(par)
        fields = (flat["c" + str(p)], edge["c" + str(p)])
        for i in range(lo, hi):
            inner = [[ref[k, 1 - par, i] for ref in refs] for k in range(3)]
            field = []
            for k in range(3):
                field.append([])
                for z in range(1 if extent == 0 else 2):
                    o, far = inner[k][z], inner[k][1 - z]
                    back = refs[z][k, 1 - par, max(i - 1, 0)]
                    ahead = refs[z][k, 1 - par, min(i + 1, 5)]
                    flipped = jnp.stack([o[1], o[0]])
                    total = o + jnp.where(opened, ahead, back)
                    total = total + shift_y(o, flipped, 1) + shift_y(o, flipped, -1)
                    total = total + shift_z(o, far, 1) + shift_z(o, far, -1)
                    field[k].append(0.5 * total + fields[z][0, par, i] * drive[z, k, par, i])
            for z in range(1 if extent == 0 else 2):
                own = [refs[z][k, par, i] for k in range(3)]
                b = [field[k][z] for k in range(3)]
                chosen = fields[z][1, par, i] == bit
                if extent == 0:
                    own, b, chosen = [v[0] for v in own], [v[0] for v in b], chosen[0]
                new = turn(own, b, twice)
                for k in range(3):
                    value = jnp.where(chosen, new[k], own[k])
                    if extent == 0:
                        refs[z][k, par, i, 0] = value
                    else:
                        refs[z][k, par, i] = value

    def pass_on(name, source):
        send(name, flat[source])
        flat[name][:, :, 2:4, 0] = flat[source][:, :, 2:4, 0]

    arrive("m1")
    drives(0, "m1")
    arrive("m0")
    arrive("c0")
    for k, sector in enumerate((0, 1, 2, 3)):
        step(0, "m0", sector, 3 - k)
    pass_on("e1", "m0")
    arrive("c1")
    for p in range(2):
        for c in copies_f(p):
            c.wait_send()
    for name in ("m1", "m0", "c0", "c1"):
        sent(name)
    arrive("e1")
    drives(1, "e1")
    for k, sector in enumerate((4, 5, 6, 7)):
        step(1, "m1", sector, 3 - k, sector == 7)
    pass_on("e2", "m1")
    sent("e1")
    arrive("e2")
    for k, sector in enumerate((6, 5, 4)):
        step(1, "e2", sector, 2 - k)
    pass_on("e3", "e2")
    sent("e2")
    arrive("e3")
    drives(0, "e3")
    for k, sector in enumerate((3, 2, 1, 0)):
        step(0, "e1", sector, 3 - k)
    for p, name in ((0, "e1"), (1, "e2")):
        for k in range(3):
            for i in range(2):
                planes = by_parity(flat[name][k, 0, 2 + i, 0], flat[name][k, 1, 2 + i, 0])
                for x in range(2):
                    mom_out[3 * p + k, 2 * i + x] = planes[x]

    sent("e3")


def on_device(displacement, velocity, moments, sector_bit, weight_in, bias_in, weight_mid, weight_out):
    given = (
        displacement, velocity, moments, sector_bit,
        weight_in, bias_in, weight_mid, weight_out.T,
    )
    vmem = pl.BlockSpec(memory_space=pltpu.VMEM)
    shape = jax.ShapeDtypeStruct(displacement.shape, F32)
    count = len(NAMES)
    groups = [pltpu.VMEM((f, 2, 6, 2, 8, 128), F32) for f in GROUPS.values()]
    return pl.pallas_call(
        kernel,
        out_shape=(shape, shape, shape),
        in_specs=[pl.BlockSpec(memory_space=pltpu.HBM)] * 8,
        out_specs=(vmem, vmem, vmem),
        scratch_shapes=groups
        + groups
        + [
            pltpu.VMEM((count, 8, 128), F32),
            pltpu.VMEM((count, 3, 2, 2, 8, 128), F32),
            pltpu.VMEM((2, 2, 8, 128), F32),
            pltpu.VMEM((2, 3, 2, 2, 8, 128), F32),
            pltpu.VMEM((2, 3, 2, 6, 2, 8, 128), F32),
            pltpu.VMEM((1024, 128), F32),
            pltpu.VMEM((256, 128), F32),
            pltpu.VMEM((256, 32), BF16),
            pltpu.VMEM((256, 256), BF16),
            pltpu.VMEM((16, 256), BF16),
            pltpu.VMEM((256, 128), F32),
        ]
        + [pltpu.VMEM(a.shape, a.dtype) for a in given]
        + [
            pltpu.SemaphoreType.DMA((len(given),)),
            pltpu.SemaphoreType.DMA((count, 2)),
            pltpu.SemaphoreType.DMA((count, 2)),
            pltpu.SemaphoreType.DMA((2, len(UP))),
            pltpu.SemaphoreType.DMA((2, len(UP))),
        ],
        compiler_params=pltpu.CompilerParams(
            collective_id=0, has_side_effects=True, vmem_limit_bytes=60 * 1024 * 1024
        ),
    )(*given)


def solution(mesh):
    cells = P(None, "gx", "gy", "gz")
    return jax.shard_map(
        on_device,
        mesh=mesh,
        in_specs=(cells, cells, cells, cells, P(), P(), P(), P()),
        out_specs=(cells, cells, cells),
        check_vma=False,
    )
```

```python
import functools
import itertools

import jax
import jax.numpy as jnp
from jax import lax
from jax.experimental import pallas as pl
from jax.experimental.pallas import tpu as pltpu
from jax.sharding import PartitionSpec as P

AXES = ("gx", "gy", "gz")
MESH = pl.DeviceIdType.MESH
F32 = jnp.float32
BF16 = jnp.bfloat16

DIRS = sorted(
    (d for d in itertools.product((-1, 0, 1), repeat=3) if d != (0, 0, 0)),
    key=lambda d: -sum(abs(c) for c in d),
)
UP = [d for d in DIRS if min(d) >= 0]
DOWN = [d for d in DIRS if max(d) <= 0]
GROUPS = {"f1": 6, "f0": 6, "m1": 3, "m0": 3, "c0": 2, "c1": 2, "e1": 3, "e2": 3, "e3": 3}
NAMES = list(GROUPS)


def kernel(
    disp_in, mom_in, bits_in, w_in_in, bias_in, w_mid_in, w_out_in,
    results,
    *scratch,
):
    n = len(NAMES)
    flat = dict(zip(NAMES, scratch[:n]))
    edge = dict(zip(NAMES, scratch[n : 2 * n]))
    strip, landed, strip_f, landed_f, drive, table, heads, w1, w2, w3, bias_wide = scratch[2 * n : 2 * n + 11]
    disp, mom, bits, w_in, bias, w_mid, w_out, in_sem, send_sem, recv_sem, send_sem_f, recv_sem_f = scratch[2 * n + 11 :]
    given = (
        (mom_in, mom), (disp_in, disp), (w_in_in, w_in), (bias_in, bias), (w_mid_in, w_mid),
        (w_out_in, w_out), (bits_in, bits),
    )
    loads = [pltpu.make_async_copy(a, b, in_sem.at[k]) for k, (a, b) in enumerate(given)]
    for load in loads:
        load.start()

    size = [lax.axis_size(a) for a in AXES]
    me = [lax.axis_index(a) for a in AXES]
    beside = [
        {-1: lax.rem(i + s - 1, s), 0: i, 1: lax.rem(i + 1, s)} for i, s in zip(me, size)
    ]

    def device(d):
        return tuple(beside[k][d[k]] for k in range(3))

    barrier = pltpu.get_barrier_semaphore()
    for d in DIRS:
        pl.semaphore_signal(barrier, inc=1, device_id=device(d), device_id_type=MESH)

    row = lax.broadcasted_iota(jnp.int32, (8, 128), 0)
    lane = lax.broadcasted_iota(jnp.int32, (8, 128), 1)
    odd = (row + lane) % 2 == 1
    behind = lane % 8 >= 4
    first_lane, last_lane = lane == 0, lane == 127
    first_row, last_row = row == 0, row == 7

    def by_parity(even_plane, odd_plane):
        return jnp.where(odd, odd_plane, even_plane), jnp.where(odd, even_plane, odd_plane)

    def pack(ref, first, fields):
        total = jnp.zeros((8, 128), F32)
        j = 0
        for f in range(fields):
            for par in range(2):
                for i in range(2):
                    turned = ref[first + f, par, 2 + i, 0]
                    if j:
                        turned = pltpu.roll(turned, 8 * j, 1)
                    total = jnp.where((lane + 4) // 8 % 16 == j, turned, total)
                    j += 1
        return total

    def send(name, source, first=0):
        g, fields = NAMES.index(name), GROUPS[name]
        strip[g] = pack(source, first, fields)
        for d in DIRS:
            rows = {0: slice(0, 8), 1: slice(4, 8), -1: slice(0, 4)}[d[1]]
            side, tile = 1 - d[0], abs(d[1])
            if d[2]:
                src = strip.at[g, rows]
                dst = landed.at[g, side, tile, (d[2] + 1) // 2, rows]
            else:
                src = source.at[first : first + fields, :, 2:4, 0, rows]
                dst = flat[name].at[:, :, 2 * side : 2 * side + 2, tile, rows]
            k = abs(d[2])
            pltpu.make_async_remote_copy(
                src_ref=src, dst_ref=dst, send_sem=send_sem.at[g, k], recv_sem=recv_sem.at[g, k],
                device_id=device(d), device_id_type=MESH,
            ).start()

    def both_waits(name, sems):
        g = NAMES.index(name)
        cells, strips = flat[name].at[:, :, 0:5], landed.at[g]
        pltpu.make_async_copy(cells, cells, sems.at[g, 0]).wait()
        pltpu.make_async_copy(strips, strips, sems.at[g, 1]).wait()

    def arrive(name):
        both_waits(name, recv_sem)
        unpack(name)

    def sent(name):
        both_waits(name, send_sem)

    def unpack(name):
        g = NAMES.index(name)
        for side in range(3):
            for tile in range(2):
                both = jnp.where(behind, landed[g, side, tile, 1], landed[g, side, tile, 0])
                j = 0
                for f in range(GROUPS[name]):
                    for par in range(2):
                        for i in range(2):
                            turned = pltpu.roll(both, 128 - 8 * j, 1) if j else both
                            edge[name][f, par, 2 * side + i, tile] = turned
                            j += 1

    def copies_f(p):
        ref = flat["f" + str(p)]
        for k, d in enumerate(UP if p else DOWN):
            rows = {0: slice(0, 8), 1: slice(4, 8), -1: slice(0, 4)}[d[1]]
            side, tile = 1 - d[0], abs(d[1])
            if d[2]:
                src, dst = strip_f.at[p, :, rows], landed_f.at[p, side, tile, :, rows]
            else:
                here = {0: slice(2, 4), 1: slice(3, 4), -1: slice(2, 3)}[d[0]]
                there = {0: slice(2, 4), 1: slice(1, 2), -1: slice(4, 5)}[d[0]]
                src, dst = ref.at[:, :, here, 0, rows], ref.at[:, :, there, tile, rows]
            yield pltpu.make_async_remote_copy(
                src_ref=src, dst_ref=dst, send_sem=send_sem_f.at[p, k], recv_sem=recv_sem_f.at[p, k],
                device_id=device(d), device_id_type=MESH,
            )

    def arrive_f(p):
        for c in copies_f(p):
            c.wait_recv()
        for side in (0, 1) if p else (1, 2):
            for tile in range(2):
                for kind in range(2):
                    got = landed_f[p, side, tile, kind]
                    j = 0
                    for f in range(3):
                        for par in range(2):
                            for i in range(2):
                                turned = pltpu.roll(got, 128 - 8 * j, 1) if j else got
                                edge["f" + str(p)][3 * kind + f, par, 2 * side + i, tile] = turned
                                j += 1

    def load_own(p):
        ref = flat["f" + str(p)]
        for kind, source in enumerate((disp, mom)):
            for f in range(3):
                for i in range(2):
                    pair = by_parity(source[3 * p + f, 2 * i], source[3 * p + f, 2 * i + 1])
                    ref[3 * kind + f, 0, 2 + i, 0] = pair[0]
                    ref[3 * kind + f, 1, 2 + i, 0] = pair[1]
            strip_f[p, kind] = pack(ref, 3 * kind, 3)

    loads[0].wait()
    loads[1].wait()
    load_own(1)
    pl.semaphore_wait(barrier, len(DIRS))
    for c in copies_f(1):
        c.start()
    load_own(0)
    for c in copies_f(0):
        c.start()
    for p in (1, 0):
        send("m" + str(p), flat["f" + str(p)], 3)
    for load in loads[2:]:
        load.wait()
    for p in range(2):
        flat["m" + str(p)][:, :, 2:4, 0] = flat["f" + str(p)][3:6, :, 2:4, 0]

    w1[...] = (w_in[...].astype(F32).T * 0.5).astype(BF16)
    w2[...] = (w_mid[...].astype(F32).T * 0.5).astype(BF16)
    w3[...] = jnp.concatenate([w_out[...].astype(F32), jnp.zeros((12, 256), F32)], 0).astype(BF16)
    bias_wide[...] = jnp.broadcast_to(bias[...].reshape(1, 256) * 0.5, (128, 256)).T

    def shift_z(near, far, sign):
        by, last = (127, last_lane) if sign > 0 else (1, first_lane)
        axis = near.ndim - 1
        return jnp.where(last, pltpu.roll(far, by, axis), pltpu.roll(near, by, axis))

    def shift_y(near, far, sign):
        by, last = (7, last_row) if sign > 0 else (1, first_row)
        axis = near.ndim - 2
        return jnp.where(last, pltpu.roll(far, by, axis), pltpu.roll(near, by, axis))

    def odd_of(par):
        return odd if par == 0 else jnp.logical_not(odd)

    def beside_x(ref, fields, par, i, sign):
        far = min(max(i + sign, 0), 5)
        here, there = ref[fields, 1 - par, i], ref[fields, 1 - par, far]
        crosses = odd_of(par) if sign > 0 else odd_of(1 - par)
        return jnp.where(crosses, there, here)

    def features(p):
        name, sign = "f" + str(1 - p), 2 * p - 1
        for i in range(2):
            pair = 2 + i
            cells = {}
            for kind in ("d", "m"):
                fields = slice(0, 3) if kind == "d" else slice(3, 6)
                for dx in range(2):
                    for par in range(2):
                        if dx:
                            near = beside_x(flat[name], fields, par, pair, sign)
                            far = beside_x(edge[name], fields, par, pair, sign)
                        else:
                            near, far = flat[name][fields, par, pair], edge[name][fields, par, pair]
                        cells[kind, dx, par, 0] = near
                        cells[kind, dx, 1 - par, 1] = shift_z(near, far, sign)
            for par in range(2):
                own_d = flat["f" + str(p)][0:3, par, pair, 0]
                own_m = flat["f" + str(p)][3:6, par, pair, 0]
                at = (par * 2 + i) * 8
                for o in range(8):
                    dx, dy, dz = o // 4, o // 2 % 2, o % 2
                    held = (par + dy) % 2
                    near_d, near_m = cells["d", dx, held, dz], cells["m", dx, held, dz]
                    if dy:
                        near_d = shift_y(near_d[:, 0], near_d[:, 1], sign)
                        near_m = shift_y(near_m[:, 0], near_m[:, 1], sign)
                    else:
                        near_d, near_m = near_d[:, 0], near_m[:, 0]
                    diff = near_d - own_d
                    for k in range(3):
                        table[pl.ds((4 * o + k) * 32 + at, 8), :] = diff[k]
                    table[pl.ds((4 * o + 3) * 32 + at, 8), :] = jnp.sum(own_m * near_m, axis=0)

    def network(p):
        @pl.loop(0, 8, unroll=8)
        def _(chunk):
            x = jnp.concatenate(
                [table[pl.ds(chunk * 4 + r, 32, stride=32), :] for r in range(4)], axis=1
            ).astype(BF16)
            wide = jnp.concatenate([bias_wide[...]] * 4, axis=1)
            h = jnp.dot(w1[...], x, preferred_element_type=F32) + wide
            h = (h + h * jnp.tanh(h)).astype(BF16)
            h = jnp.dot(w2[...], h, preferred_element_type=F32)
            h = (h + h * jnp.tanh(h)).astype(BF16)
            h = jnp.dot(w3[...], h, preferred_element_type=F32)
            for r in range(4):
                heads[pl.ds((chunk * 4 + r) * 8, 8), :] = h[0:8, 128 * r : 128 * r + 128]

        def head(k, par, i):
            return heads[pl.ds((par * 2 + i) * 64 + k, 8, stride=8), :]

        name = "c" + str(p)
        for i in range(2):
            for k in range(3):
                planes = by_parity(head(k, 0, i), head(k, 1, i))
                for x in range(2):
                    results[3 * p + k, 2 * i + x] = planes[x]
            for par in range(2):
                flat[name][0, par, 2 + i, 0] = 1.0 + 0.5 * jnp.tanh(head(3, par, i))
            pair = by_parity(bits[p, 2 * i].astype(F32), bits[p, 2 * i + 1].astype(F32))
            for par in range(2):
                flat[name][1, par, 2 + i, 0] = pair[par]
        send(name, flat[name])

    arrive_f(1)
    features(0)
    network(0)
    arrive_f(0)
    features(1)
    network(1)

    def drives(p, source):
        sign = 2 * p - 1

        def body(i):
            for k in range(3):
                along = []
                for par in range(2):
                    along.append([])
                    for ref in (flat[source], edge[source]):
                        far = min(max(i + sign, 0), 5)
                        crosses = odd_of(par) if sign > 0 else odd_of(1 - par)
                        other = jnp.where(crosses, ref[k, 1 - par, far], ref[k, 1 - par, i])
                        along[par].append(ref[k, par, i] + other)
                tall = []
                for par in range(2):
                    tall.append([])
                    for z in range(2):
                        o = along[1 - par][z]
                        s = shift_y(o, jnp.stack([o[1], o[0]]), sign)
                        tall[par].append(along[par][z] + s)
                for par in range(2):
                    near = tall[par][0] + shift_z(tall[1 - par][0], tall[1 - par][1], sign)
                    beyond = tall[par][1] + shift_z(tall[1 - par][1], tall[1 - par][0], sign)
                    drive[0, k, par, i] = near
                    drive[1, k, par, i] = beyond

        for i in range(6):
            body(i)

    def turn(v, b, twice):
        square = b[0] * b[0] + b[1] * b[1] + b[2] * b[2]
        z = square * (0.0025 / 64.0)
        c = 1.0 + z * (-1 / 2 + z * (1 / 24 + z * (-1 / 720 + z * (1 / 40320 - z / 3628800))))
        s = 0.05 + z * (-0.05 / 6 + z * (0.05 / 120 + z * (-0.05 / 5040 + z * (0.05 / 362880))))
        for _ in range(3):
            s = s * c
            c = 2.0 * (c * c) - 1.0
        if twice:
            s = 2.0 * (s * c)
            c = 2.0 * (c * c) - 1.0
        q = [s * b[k] for k in range(3)]
        w = [v[k] + v[k] for k in range(3)]
        t = [q[1] * w[2] - q[2] * w[1], q[2] * w[0] - q[0] * w[2], q[0] * w[1] - q[1] * w[0]]
        r = [q[1] * t[2] - q[2] * t[1], q[2] * t[0] - q[0] * t[2], q[0] * t[1] - q[1] * t[0]]
        return [v[k] + (c * t[k] + r[k]) for k in range(3)]

    def step(p, name, sector, extent, twice=False):
        par, bit = sector % 2, float(sector // 2 % 2)
        lo, hi = {3: (0, 6), 2: (1, 5), 1: (1, 5), 0: (2, 4)}[extent]
        refs = (flat[name], edge[name])
        opened = odd_of(par)
        fields = (flat["c" + str(p)], edge["c" + str(p)])
        for i in range(lo, hi):
            inner = [[ref[k, 1 - par, i] for ref in refs] for k in range(3)]
            field = []
            for k in range(3):
                field.append([])
                for z in range(1 if extent == 0 else 2):
                    o, far = inner[k][z], inner[k][1 - z]
                    back = refs[z][k, 1 - par, max(i - 1, 0)]
                    ahead = refs[z][k, 1 - par, min(i + 1, 5)]
                    flipped = jnp.stack([o[1], o[0]])
                    total = o + jnp.where(opened, ahead, back)
                    total = total + shift_y(o, flipped, 1) + shift_y(o, flipped, -1)
                    total = total + shift_z(o, far, 1) + shift_z(o, far, -1)
                    field[k].append(0.5 * total + fields[z][0, par, i] * drive[z, k, par, i])
            for z in range(1 if extent == 0 else 2):
                own = [refs[z][k, par, i] for k in range(3)]
                b = [field[k][z] for k in range(3)]
                chosen = fields[z][1, par, i] == bit
                if extent == 0:
                    own, b, chosen = [v[0] for v in own], [v[0] for v in b], chosen[0]
                new = turn(own, b, twice)
                for k in range(3):
                    value = jnp.where(chosen, new[k], own[k])
                    if extent == 0:
                        refs[z][k, par, i, 0] = value
                    else:
                        refs[z][k, par, i] = value

    def pass_on(name, source):
        send(name, flat[source])
        flat[name][:, :, 2:4, 0] = flat[source][:, :, 2:4, 0]

    arrive("m1")
    drives(0, "m1")
    arrive("m0")
    arrive("c0")
    for k, sector in enumerate((0, 1, 2, 3)):
        step(0, "m0", sector, 3 - k)
    pass_on("e1", "m0")
    arrive("c1")
    for p in range(2):
        for c in copies_f(p):
            c.wait_send()
    for name in ("m1", "m0", "c0", "c1"):
        sent(name)
    arrive("e1")
    drives(1, "e1")
    for k, sector in enumerate((4, 5, 6, 7)):
        step(1, "m1", sector, 3 - k, sector == 7)
    pass_on("e2", "m1")
    sent("e1")
    arrive("e2")
    for k, sector in enumerate((6, 5, 4)):
        step(1, "e2", sector, 2 - k)
    pass_on("e3", "e2")
    sent("e2")
    arrive("e3")
    drives(0, "e3")
    for k, sector in enumerate((3, 2, 1, 0)):
        step(0, "e1", sector, 3 - k)
    for p, name in ((0, "e1"), (1, "e2")):
        for k in range(3):
            for i in range(2):
                planes = by_parity(flat[name][k, 0, 2 + i, 0], flat[name][k, 1, 2 + i, 0])
                for x in range(2):
                    results[6 + 3 * p + k, 2 * i + x] = planes[x]

    sent("e3")


def on_device(displacement, velocity, moments, sector_bit, weight_in, bias_in, weight_mid, weight_out):
    given = (
        displacement, moments, sector_bit,
        weight_in, bias_in, weight_mid, weight_out.T,
    )
    vmem = pl.BlockSpec(memory_space=pltpu.VMEM)
    shape = jax.ShapeDtypeStruct(displacement.shape, F32)
    count = len(NAMES)
    groups = [pltpu.VMEM((f, 2, 6, 2, 8, 128), F32) for f in GROUPS.values()]
    results = pl.pallas_call(
        kernel,
        out_shape=jax.ShapeDtypeStruct((12,) + displacement.shape[1:], F32),
        in_specs=[pl.BlockSpec(memory_space=pltpu.HBM)] * 7,
        out_specs=vmem,
        scratch_shapes=groups
        + groups
        + [
            pltpu.VMEM((count, 8, 128), F32),
            pltpu.VMEM((count, 3, 2, 2, 8, 128), F32),
            pltpu.VMEM((2, 2, 8, 128), F32),
            pltpu.VMEM((2, 3, 2, 2, 8, 128), F32),
            pltpu.VMEM((2, 3, 2, 6, 2, 8, 128), F32),
            pltpu.VMEM((1024, 128), F32),
            pltpu.VMEM((256, 128), F32),
            pltpu.VMEM((256, 32), BF16),
            pltpu.VMEM((256, 256), BF16),
            pltpu.VMEM((16, 256), BF16),
            pltpu.VMEM((256, 128), F32),
        ]
        + [pltpu.VMEM(a.shape, a.dtype) for a in given]
        + [
            pltpu.SemaphoreType.DMA((len(given),)),
            pltpu.SemaphoreType.DMA((count, 2)),
            pltpu.SemaphoreType.DMA((count, 2)),
            pltpu.SemaphoreType.DMA((2, len(UP))),
            pltpu.SemaphoreType.DMA((2, len(UP))),
        ],
        compiler_params=pltpu.CompilerParams(
            collective_id=0, has_side_effects=True, vmem_limit_bytes=60 * 1024 * 1024
        ),
    )(*given)
    velocity_out = velocity + 0.25 * results[:6]
    return displacement + 0.25 * velocity_out, velocity_out, results[6:]


def solution(mesh):
    cells = P(None, "gx", "gy", "gz")
    return jax.shard_map(
        on_device,
        mesh=mesh,
        in_specs=(cells, cells, cells, cells, P(), P(), P(), P()),
        out_specs=(cells, cells, cells),
        check_vma=False,
    )
```

```python
import functools
import itertools

import jax
import jax.numpy as jnp
from jax import lax
from jax.experimental import pallas as pl
from jax.experimental.pallas import tpu as pltpu
from jax.sharding import PartitionSpec as P

AXES = ("gx", "gy", "gz")
MESH = pl.DeviceIdType.MESH
F32 = jnp.float32
BF16 = jnp.bfloat16

DIRS = sorted(
    (d for d in itertools.product((-1, 0, 1), repeat=3) if d != (0, 0, 0)),
    key=lambda d: -sum(abs(c) for c in d),
)
UP = [d for d in DIRS if min(d) >= 0]
DOWN = [d for d in DIRS if max(d) <= 0]
GROUPS = {"f1": 6, "f0": 6, "m1": 3, "m0": 3, "c0": 2, "c1": 2, "e1": 3, "e2": 3, "e3": 3}
NAMES = list(GROUPS)


def kernel(
    disp_in, mom_in, bits_in, w_in_in, bias_in, w_mid_in, w_out_in,
    results,
    *scratch,
):
    n = len(NAMES)
    flat = dict(zip(NAMES, scratch[:n]))
    edge = dict(zip(NAMES, scratch[n : 2 * n]))
    strip, landed, strip_f, landed_f, drive, table, heads, w1, w2, w3, bias_wide = scratch[2 * n : 2 * n + 11]
    disp, mom, bits, w_in, bias, w_mid, w_out, in_sem, send_sem, recv_sem, send_sem_f, recv_sem_f = scratch[2 * n + 11 :]
    given = (
        (mom_in, mom), (disp_in, disp), (w_in_in, w_in), (bias_in, bias), (w_mid_in, w_mid),
        (w_out_in, w_out), (bits_in, bits),
    )
    loads = [pltpu.make_async_copy(a, b, in_sem.at[k]) for k, (a, b) in enumerate(given)]
    for load in loads:
        load.start()

    size = [lax.axis_size(a) for a in AXES]
    me = [lax.axis_index(a) for a in AXES]
    beside = [
        {-1: lax.rem(i + s - 1, s), 0: i, 1: lax.rem(i + 1, s)} for i, s in zip(me, size)
    ]

    def device(d):
        return tuple(beside[k][d[k]] for k in range(3))

    barrier = pltpu.get_barrier_semaphore()
    for d in DIRS:
        pl.semaphore_signal(barrier, inc=1, device_id=device(d), device_id_type=MESH)

    row = lax.broadcasted_iota(jnp.int32, (8, 128), 0)
    lane = lax.broadcasted_iota(jnp.int32, (8, 128), 1)
    odd = (row + lane) % 2 == 1
    behind = lane % 8 >= 4
    first_lane, last_lane = lane == 0, lane == 127
    first_row, last_row = row == 0, row == 7

    def by_parity(even_plane, odd_plane):
        return jnp.where(odd, odd_plane, even_plane), jnp.where(odd, even_plane, odd_plane)

    def pack(ref, first, fields):
        total = jnp.zeros((8, 128), F32)
        j = 0
        for f in range(fields):
            for par in range(2):
                for i in range(2):
                    turned = ref[first + f, par, 2 + i, 0]
                    if j:
                        turned = pltpu.roll(turned, 8 * j, 1)
                    total = jnp.where((lane + 4) // 8 % 16 == j, turned, total)
                    j += 1
        return total

    def send(name, source, first=0):
        g, fields = NAMES.index(name), GROUPS[name]
        strip[g] = pack(source, first, fields)
        for d in DIRS:
            rows = {0: slice(0, 8), 1: slice(4, 8), -1: slice(0, 4)}[d[1]]
            side, tile = 1 - d[0], abs(d[1])
            if d[2]:
                src = strip.at[g, rows]
                dst = landed.at[g, side, tile, (d[2] + 1) // 2, rows]
            else:
                src = source.at[first : first + fields, :, 2:4, 0, rows]
                dst = flat[name].at[:, :, 2 * side : 2 * side + 2, tile, rows]
            k = abs(d[2])
            pltpu.make_async_remote_copy(
                src_ref=src, dst_ref=dst, send_sem=send_sem.at[g, k], recv_sem=recv_sem.at[g, k],
                device_id=device(d), device_id_type=MESH,
            ).start()

    def both_waits(name, sems):
        g = NAMES.index(name)
        cells, strips = flat[name].at[:, :, 0:5], landed.at[g]
        pltpu.make_async_copy(cells, cells, sems.at[g, 0]).wait()
        pltpu.make_async_copy(strips, strips, sems.at[g, 1]).wait()

    def arrive(name):
        both_waits(name, recv_sem)
        unpack(name)

    def sent(name):
        both_waits(name, send_sem)

    def unpack(name):
        g = NAMES.index(name)
        for side in range(3):
            for tile in range(2):
                both = jnp.where(behind, landed[g, side, tile, 1], landed[g, side, tile, 0])
                j = 0
                for f in range(GROUPS[name]):
                    for par in range(2):
                        for i in range(2):
                            turned = pltpu.roll(both, 128 - 8 * j, 1) if j else both
                            edge[name][f, par, 2 * side + i, tile] = turned
                            j += 1

    def copies_f(p):
        ref = flat["f" + str(p)]
        for k, d in enumerate(UP if p else DOWN):
            rows = {0: slice(0, 8), 1: slice(4, 8), -1: slice(0, 4)}[d[1]]
            side, tile = 1 - d[0], abs(d[1])
            if d[2]:
                src, dst = strip_f.at[p, :, rows], landed_f.at[p, side, tile, :, rows]
            else:
                here = {0: slice(2, 4), 1: slice(3, 4), -1: slice(2, 3)}[d[0]]
                there = {0: slice(2, 4), 1: slice(1, 2), -1: slice(4, 5)}[d[0]]
                src, dst = ref.at[:, :, here, 0, rows], ref.at[:, :, there, tile, rows]
            yield pltpu.make_async_remote_copy(
                src_ref=src, dst_ref=dst, send_sem=send_sem_f.at[p, k], recv_sem=recv_sem_f.at[p, k],
                device_id=device(d), device_id_type=MESH,
            )

    def arrive_f(p):
        for c in copies_f(p):
            c.wait_recv()
        for side in (0, 1) if p else (1, 2):
            for tile in range(2):
                for kind in range(2):
                    got = landed_f[p, side, tile, kind]
                    j = 0
                    for f in range(3):
                        for par in range(2):
                            for i in range(2):
                                turned = pltpu.roll(got, 128 - 8 * j, 1) if j else got
                                edge["f" + str(p)][3 * kind + f, par, 2 * side + i, tile] = turned
                                j += 1

    def load_own(p):
        ref = flat["f" + str(p)]
        for kind, source in enumerate((disp, mom)):
            for f in range(3):
                for i in range(2):
                    pair = by_parity(source[3 * p + f, 2 * i], source[3 * p + f, 2 * i + 1])
                    ref[3 * kind + f, 0, 2 + i, 0] = pair[0]
                    ref[3 * kind + f, 1, 2 + i, 0] = pair[1]
            strip_f[p, kind] = pack(ref, 3 * kind, 3)

    loads[0].wait()
    loads[1].wait()
    load_own(1)
    pl.semaphore_wait(barrier, len(DIRS))
    for c in copies_f(1):
        c.start()
    load_own(0)
    for c in copies_f(0):
        c.start()
    for p in (1, 0):
        send("m" + str(p), flat["f" + str(p)], 3)
    for load in loads[2:]:
        load.wait()
    for p in range(2):
        flat["m" + str(p)][:, :, 2:4, 0] = flat["f" + str(p)][3:6, :, 2:4, 0]

    w1[...] = (w_in[...].astype(F32).T * 0.5).astype(BF16)
    w2[...] = (w_mid[...].astype(F32).T * 0.5).astype(BF16)
    w3[...] = jnp.concatenate([w_out[...].astype(F32), jnp.zeros((12, 256), F32)], 0).astype(BF16)
    bias_wide[...] = jnp.broadcast_to(bias[...].reshape(1, 256) * 0.5, (128, 256)).T

    def shift_z(near, far, sign):
        by, last = (127, last_lane) if sign > 0 else (1, first_lane)
        axis = near.ndim - 1
        return jnp.where(last, pltpu.roll(far, by, axis), pltpu.roll(near, by, axis))

    def shift_y(near, far, sign):
        by, last = (7, last_row) if sign > 0 else (1, first_row)
        axis = near.ndim - 2
        return jnp.where(last, pltpu.roll(far, by, axis), pltpu.roll(near, by, axis))

    def wrap_y(cells, sign):
        by, last = (7, last_row) if sign > 0 else (1, first_row)
        turned = pltpu.roll(cells, by, 1)
        return jnp.where(last, jnp.stack([turned[1], turned[0]]), turned)

    def wrap_z(pair, sign):
        by, last = (127, last_lane) if sign > 0 else (1, first_lane)
        turned = [pltpu.roll(v, by, 2) for v in pair]
        return [jnp.where(last, turned[1 - z], turned[z]) for z in range(2)]

    def odd_of(par):
        return odd if par == 0 else jnp.logical_not(odd)

    def beside_x(ref, fields, par, i, sign):
        far = min(max(i + sign, 0), 5)
        here, there = ref[fields, 1 - par, i], ref[fields, 1 - par, far]
        crosses = odd_of(par) if sign > 0 else odd_of(1 - par)
        return jnp.where(crosses, there, here)

    def features(p):
        name, sign = "f" + str(1 - p), 2 * p - 1
        for i in range(2):
            pair = 2 + i
            cells = {}
            for kind in ("d", "m"):
                fields = slice(0, 3) if kind == "d" else slice(3, 6)
                for dx in range(2):
                    for par in range(2):
                        if dx:
                            near = beside_x(flat[name], fields, par, pair, sign)
                            far = beside_x(edge[name], fields, par, pair, sign)
                        else:
                            near, far = flat[name][fields, par, pair], edge[name][fields, par, pair]
                        cells[kind, dx, par, 0] = near
                        cells[kind, dx, 1 - par, 1] = shift_z(near, far, sign)
            for par in range(2):
                own_d = flat["f" + str(p)][0:3, par, pair, 0]
                own_m = flat["f" + str(p)][3:6, par, pair, 0]
                at = (par * 2 + i) * 8
                for o in range(8):
                    dx, dy, dz = o // 4, o // 2 % 2, o % 2
                    held = (par + dy) % 2
                    near_d, near_m = cells["d", dx, held, dz], cells["m", dx, held, dz]
                    if dy:
                        near_d = shift_y(near_d[:, 0], near_d[:, 1], sign)
                        near_m = shift_y(near_m[:, 0], near_m[:, 1], sign)
                    else:
                        near_d, near_m = near_d[:, 0], near_m[:, 0]
                    diff = near_d - own_d
                    for k in range(3):
                        table[pl.ds((4 * o + k) * 32 + at, 8), :] = diff[k]
                    table[pl.ds((4 * o + 3) * 32 + at, 8), :] = jnp.sum(own_m * near_m, axis=0)

    def network(p):
        @pl.loop(0, 4, unroll=4)
        def _(chunk):
            x = jnp.concatenate(
                [table[pl.ds(chunk * 8 + r, 32, stride=32), :] for r in range(8)], axis=1
            ).astype(BF16)
            wide = jnp.concatenate([bias_wide[...]] * 8, axis=1)
            h = jnp.dot(w1[...], x, preferred_element_type=F32) + wide
            h = (h + h * jnp.tanh(h)).astype(BF16)
            h = jnp.dot(w2[...], h, preferred_element_type=F32)
            h = (h + h * jnp.tanh(h)).astype(BF16)
            h = jnp.dot(w3[...], h, preferred_element_type=F32)
            for r in range(8):
                heads[pl.ds((chunk * 8 + r) * 8, 8), :] = h[0:8, 128 * r : 128 * r + 128]

        def head(k, par, i):
            return heads[pl.ds((par * 2 + i) * 64 + k, 8, stride=8), :]

        name = "c" + str(p)
        for i in range(2):
            for k in range(3):
                planes = by_parity(head(k, 0, i), head(k, 1, i))
                for x in range(2):
                    results[3 * p + k, 2 * i + x] = planes[x]
            for par in range(2):
                flat[name][0, par, 2 + i, 0] = 1.0 + 0.5 * jnp.tanh(head(3, par, i))
            pair = by_parity(bits[p, 2 * i].astype(F32), bits[p, 2 * i + 1].astype(F32))
            for par in range(2):
                flat[name][1, par, 2 + i, 0] = pair[par]
        send(name, flat[name])

    arrive_f(1)
    features(0)
    network(0)
    arrive_f(0)
    features(1)
    network(1)

    def drives(p, source):
        sign = 2 * p - 1

        def body(i):
            for k in range(3):
                along = []
                for par in range(2):
                    along.append([])
                    for ref in (flat[source], edge[source]):
                        far = min(max(i + sign, 0), 5)
                        crosses = odd_of(par) if sign > 0 else odd_of(1 - par)
                        other = jnp.where(crosses, ref[k, 1 - par, far], ref[k, 1 - par, i])
                        along[par].append(ref[k, par, i] + other)
                tall = []
                for par in range(2):
                    tall.append([])
                    for z in range(2):
                        tall[par].append(along[par][z] + wrap_y(along[1 - par][z], sign))
                for par in range(2):
                    other = wrap_z(tall[1 - par], sign)
                    for z in range(2):
                        drive[z, k, par, i] = tall[par][z] + other[z]

        for i in range(6):
            body(i)

    def turn(v, b, twice):
        square = b[0] * b[0] + b[1] * b[1] + b[2] * b[2]
        z = square * (0.0025 / 64.0)
        c = 1.0 + z * (-1 / 2 + z * (1 / 24 + z * (-1 / 720 + z * (1 / 40320 - z / 3628800))))
        s = 0.05 + z * (-0.05 / 6 + z * (0.05 / 120 + z * (-0.05 / 5040 + z * (0.05 / 362880))))
        for _ in range(3):
            s = s * c
            c = 2.0 * (c * c) - 1.0
        if twice:
            s = 2.0 * (s * c)
            c = 2.0 * (c * c) - 1.0
        q = [s * b[k] for k in range(3)]
        w = [v[k] + v[k] for k in range(3)]
        t = [q[1] * w[2] - q[2] * w[1], q[2] * w[0] - q[0] * w[2], q[0] * w[1] - q[1] * w[0]]
        r = [q[1] * t[2] - q[2] * t[1], q[2] * t[0] - q[0] * t[2], q[0] * t[1] - q[1] * t[0]]
        return [v[k] + (c * t[k] + r[k]) for k in range(3)]

    def step(p, name, sector, extent, twice=False):
        par, bit = sector % 2, float(sector // 2 % 2)
        lo, hi = {3: (0, 6), 2: (1, 5), 1: (1, 5), 0: (2, 4)}[extent]
        refs = (flat[name], edge[name])
        opened = odd_of(par)
        fields = (flat["c" + str(p)], edge["c" + str(p)])
        for i in range(lo, hi):
            inner = [[ref[k, 1 - par, i] for ref in refs] for k in range(3)]
            field = []
            for k in range(3):
                field.append([])
                up, down = wrap_z(inner[k], 1), wrap_z(inner[k], -1)
                for z in range(1 if extent == 0 else 2):
                    o = inner[k][z]
                    back = refs[z][k, 1 - par, max(i - 1, 0)]
                    ahead = refs[z][k, 1 - par, min(i + 1, 5)]
                    total = o + jnp.where(opened, ahead, back)
                    total = total + (wrap_y(o, 1) + wrap_y(o, -1)) + (up[z] + down[z])
                    field[k].append(0.5 * total + fields[z][0, par, i] * drive[z, k, par, i])
            for z in range(1 if extent == 0 else 2):
                own = [refs[z][k, par, i] for k in range(3)]
                b = [field[k][z] for k in range(3)]
                chosen = fields[z][1, par, i] == bit
                if extent == 0:
                    own, b, chosen = [v[0] for v in own], [v[0] for v in b], chosen[0]
                new = turn(own, b, twice)
                for k in range(3):
                    value = jnp.where(chosen, new[k], own[k])
                    if extent == 0:
                        refs[z][k, par, i, 0] = value
                    else:
                        refs[z][k, par, i] = value

    def pass_on(name, source):
        send(name, flat[source])
        flat[name][:, :, 2:4, 0] = flat[source][:, :, 2:4, 0]

    arrive("m1")
    drives(0, "m1")
    arrive("m0")
    arrive("c0")
    for k, sector in enumerate((0, 1, 2, 3)):
        step(0, "m0", sector, 3 - k)
    pass_on("e1", "m0")
    arrive("c1")
    for p in range(2):
        for c in copies_f(p):
            c.wait_send()
    for name in ("m1", "m0", "c0", "c1"):
        sent(name)
    arrive("e1")
    drives(1, "e1")
    for k, sector in enumerate((4, 5, 6, 7)):
        step(1, "m1", sector, 3 - k, sector == 7)
    pass_on("e2", "m1")
    sent("e1")
    arrive("e2")
    for k, sector in enumerate((6, 5, 4)):
        step(1, "e2", sector, 2 - k)
    pass_on("e3", "e2")
    sent("e2")
    arrive("e3")
    drives(0, "e3")
    for k, sector in enumerate((3, 2, 1, 0)):
        step(0, "e1", sector, 3 - k)
    for p, name in ((0, "e1"), (1, "e2")):
        for k in range(3):
            for i in range(2):
                planes = by_parity(flat[name][k, 0, 2 + i, 0], flat[name][k, 1, 2 + i, 0])
                for x in range(2):
                    results[6 + 3 * p + k, 2 * i + x] = planes[x]

    sent("e3")


def on_device(displacement, velocity, moments, sector_bit, weight_in, bias_in, weight_mid, weight_out):
    given = (
        displacement, moments, sector_bit,
        weight_in, bias_in, weight_mid, weight_out.T,
    )
    vmem = pl.BlockSpec(memory_space=pltpu.VMEM)
    shape = jax.ShapeDtypeStruct(displacement.shape, F32)
    count = len(NAMES)
    groups = [pltpu.VMEM((f, 2, 6, 2, 8, 128), F32) for f in GROUPS.values()]
    results = pl.pallas_call(
        kernel,
        out_shape=jax.ShapeDtypeStruct((12,) + displacement.shape[1:], F32),
        in_specs=[pl.BlockSpec(memory_space=pltpu.HBM)] * 7,
        out_specs=vmem,
        scratch_shapes=groups
        + groups
        + [
            pltpu.VMEM((count, 8, 128), F32),
            pltpu.VMEM((count, 3, 2, 2, 8, 128), F32),
            pltpu.VMEM((2, 2, 8, 128), F32),
            pltpu.VMEM((2, 3, 2, 2, 8, 128), F32),
            pltpu.VMEM((2, 3, 2, 6, 2, 8, 128), F32),
            pltpu.VMEM((1024, 128), F32),
            pltpu.VMEM((256, 128), F32),
            pltpu.VMEM((256, 32), BF16),
            pltpu.VMEM((256, 256), BF16),
            pltpu.VMEM((16, 256), BF16),
            pltpu.VMEM((256, 128), F32),
        ]
        + [pltpu.VMEM(a.shape, a.dtype) for a in given]
        + [
            pltpu.SemaphoreType.DMA((len(given),)),
            pltpu.SemaphoreType.DMA((count, 2)),
            pltpu.SemaphoreType.DMA((count, 2)),
            pltpu.SemaphoreType.DMA((2, len(UP))),
            pltpu.SemaphoreType.DMA((2, len(UP))),
        ],
        compiler_params=pltpu.CompilerParams(
            collective_id=0, has_side_effects=True, vmem_limit_bytes=60 * 1024 * 1024
        ),
    )(*given)
    velocity_out = velocity + 0.25 * results[:6]
    return displacement + 0.25 * velocity_out, velocity_out, results[6:]


def solution(mesh):
    cells = P(None, "gx", "gy", "gz")
    return jax.shard_map(
        on_device,
        mesh=mesh,
        in_specs=(cells, cells, cells, cells, P(), P(), P(), P()),
        out_specs=(cells, cells, cells),
        check_vma=False,
    )
```

```python
import functools
import itertools

import jax
import jax.numpy as jnp
from jax import lax
from jax.experimental import pallas as pl
from jax.experimental.pallas import tpu as pltpu
from jax.sharding import PartitionSpec as P

AXES = ("gx", "gy", "gz")
MESH = pl.DeviceIdType.MESH
F32 = jnp.float32
BF16 = jnp.bfloat16

DIRS = sorted(
    (d for d in itertools.product((-1, 0, 1), repeat=3) if d != (0, 0, 0)),
    key=lambda d: -sum(abs(c) for c in d),
)
UP = [d for d in DIRS if min(d) >= 0]
DOWN = [d for d in DIRS if max(d) <= 0]
GROUPS = {"f1": 6, "f0": 6, "m1": 3, "m0": 3, "c0": 2, "c1": 2, "e1": 3, "e2": 3, "e3": 3}
NAMES = list(GROUPS)


def kernel(
    disp_in, mom_in, bits_in, w_in_in, bias_in, w_mid_in, w_out_in,
    results,
    *scratch,
):
    n = len(NAMES)
    flat = dict(zip(NAMES, scratch[:n]))
    edge = dict(zip(NAMES, scratch[n : 2 * n]))
    strip, landed, strip_f, landed_f, drive, table, heads, w1, w2, w3, bias_wide = scratch[2 * n : 2 * n + 11]
    disp, mom, bits, w_in, bias, w_mid, w_out, in_sem, send_sem, recv_sem, send_sem_f, recv_sem_f = scratch[2 * n + 11 :]
    given = (
        (mom_in, mom), (disp_in, disp), (w_in_in, w_in), (bias_in, bias), (w_mid_in, w_mid),
        (w_out_in, w_out), (bits_in, bits),
    )
    loads = [pltpu.make_async_copy(a, b, in_sem.at[k]) for k, (a, b) in enumerate(given)]

    size = [lax.axis_size(a) for a in AXES]
    me = [lax.axis_index(a) for a in AXES]
    beside = [
        {-1: lax.rem(i + s - 1, s), 0: i, 1: lax.rem(i + 1, s)} for i, s in zip(me, size)
    ]

    def device(d):
        return tuple(beside[k][d[k]] for k in range(3))

    barrier = pltpu.get_barrier_semaphore()
    for d in DIRS:
        pl.semaphore_signal(barrier, inc=1, device_id=device(d), device_id_type=MESH)
    for load in loads:
        load.start()

    row = lax.broadcasted_iota(jnp.int32, (8, 128), 0)
    lane = lax.broadcasted_iota(jnp.int32, (8, 128), 1)
    odd = (row + lane) % 2 == 1
    behind = lane % 8 >= 4
    first_lane, last_lane = lane == 0, lane == 127
    first_row, last_row = row == 0, row == 7

    def by_parity(even_plane, odd_plane):
        return jnp.where(odd, odd_plane, even_plane), jnp.where(odd, even_plane, odd_plane)

    def pack(ref, first, fields):
        total = jnp.zeros((8, 128), F32)
        j = 0
        for f in range(fields):
            for par in range(2):
                for i in range(2):
                    turned = ref[first + f, par, 2 + i, 0]
                    if j:
                        turned = pltpu.roll(turned, 8 * j, 1)
                    total = jnp.where((lane + 4) // 8 % 16 == j, turned, total)
                    j += 1
        return total

    def send(name, source, first=0):
        g, fields = NAMES.index(name), GROUPS[name]
        strip[g] = pack(source, first, fields)
        for d in DIRS:
            rows = {0: slice(0, 8), 1: slice(4, 8), -1: slice(0, 4)}[d[1]]
            side, tile = 1 - d[0], abs(d[1])
            if d[2]:
                src = strip.at[g, rows]
                dst = landed.at[g, side, tile, (d[2] + 1) // 2, rows]
            else:
                src = source.at[first : first + fields, :, 2:4, 0, rows]
                dst = flat[name].at[:, :, 2 * side : 2 * side + 2, tile, rows]
            k = abs(d[2])
            pltpu.make_async_remote_copy(
                src_ref=src, dst_ref=dst, send_sem=send_sem.at[g, k], recv_sem=recv_sem.at[g, k],
                device_id=device(d), device_id_type=MESH,
            ).start()

    def both_waits(name, sems):
        g = NAMES.index(name)
        cells, strips = flat[name].at[:, :, 0:5], landed.at[g]
        pltpu.make_async_copy(cells, cells, sems.at[g, 0]).wait()
        pltpu.make_async_copy(strips, strips, sems.at[g, 1]).wait()

    def arrive(name):
        both_waits(name, recv_sem)
        unpack(name)

    def sent(name):
        both_waits(name, send_sem)

    def unpack(name):
        g = NAMES.index(name)
        for side in range(3):
            for tile in range(2):
                both = jnp.where(behind, landed[g, side, tile, 1], landed[g, side, tile, 0])
                j = 0
                for f in range(GROUPS[name]):
                    for par in range(2):
                        for i in range(2):
                            turned = pltpu.roll(both, 128 - 8 * j, 1) if j else both
                            edge[name][f, par, 2 * side + i, tile] = turned
                            j += 1

    def copies_f(p):
        ref = flat["f" + str(p)]
        for k, d in enumerate(UP if p else DOWN):
            rows = {0: slice(0, 8), 1: slice(4, 8), -1: slice(0, 4)}[d[1]]
            side, tile = 1 - d[0], abs(d[1])
            if d[2]:
                src, dst = strip_f.at[p, :, rows], landed_f.at[p, side, tile, :, rows]
            else:
                here = {0: slice(2, 4), 1: slice(3, 4), -1: slice(2, 3)}[d[0]]
                there = {0: slice(2, 4), 1: slice(1, 2), -1: slice(4, 5)}[d[0]]
                src, dst = ref.at[:, :, here, 0, rows], ref.at[:, :, there, tile, rows]
            yield pltpu.make_async_remote_copy(
                src_ref=src, dst_ref=dst, send_sem=send_sem_f.at[p, k], recv_sem=recv_sem_f.at[p, k],
                device_id=device(d), device_id_type=MESH,
            )

    def arrive_f(p):
        for c in copies_f(p):
            c.wait_recv()
        for side in (0, 1) if p else (1, 2):
            for tile in range(2):
                for kind in range(2):
                    got = landed_f[p, side, tile, kind]
                    j = 0
                    for f in range(3):
                        for par in range(2):
                            for i in range(2):
                                turned = pltpu.roll(got, 128 - 8 * j, 1) if j else got
                                edge["f" + str(p)][3 * kind + f, par, 2 * side + i, tile] = turned
                                j += 1

    def load_own(p):
        ref = flat["f" + str(p)]
        for kind, source in enumerate((disp, mom)):
            for f in range(3):
                for i in range(2):
                    pair = by_parity(source[3 * p + f, 2 * i], source[3 * p + f, 2 * i + 1])
                    ref[3 * kind + f, 0, 2 + i, 0] = pair[0]
                    ref[3 * kind + f, 1, 2 + i, 0] = pair[1]
            strip_f[p, kind] = pack(ref, 3 * kind, 3)

    loads[0].wait()
    loads[1].wait()
    load_own(1)
    pl.semaphore_wait(barrier, len(DIRS))
    for c in copies_f(1):
        c.start()
    load_own(0)
    for c in copies_f(0):
        c.start()
    for p in (1, 0):
        send("m" + str(p), flat["f" + str(p)], 3)
    for load in loads[2:]:
        load.wait()
    for p in range(2):
        flat["m" + str(p)][:, :, 2:4, 0] = flat["f" + str(p)][3:6, :, 2:4, 0]
        for i in range(2):
            pair = by_parity(bits[p, 2 * i].astype(F32), bits[p, 2 * i + 1].astype(F32))
            for par in range(2):
                flat["c" + str(p)][1, par, 2 + i, 0] = pair[par]

    w1[...] = (w_in[...].astype(F32).T * 0.5).astype(BF16)
    w2[...] = (w_mid[...].astype(F32).T * 0.5).astype(BF16)
    w3[...] = jnp.concatenate([w_out[...].astype(F32), jnp.zeros((12, 256), F32)], 0).astype(BF16)
    bias_wide[...] = jnp.broadcast_to(bias[...].reshape(1, 256) * 0.5, (128, 256)).T

    def shift_z(near, far, sign):
        by, last = (127, last_lane) if sign > 0 else (1, first_lane)
        axis = near.ndim - 1
        return jnp.where(last, pltpu.roll(far, by, axis), pltpu.roll(near, by, axis))

    def shift_y(near, far, sign):
        by, last = (7, last_row) if sign > 0 else (1, first_row)
        axis = near.ndim - 2
        return jnp.where(last, pltpu.roll(far, by, axis), pltpu.roll(near, by, axis))

    def wrap_y(cells, sign):
        by, last = (7, last_row) if sign > 0 else (1, first_row)
        turned = pltpu.roll(cells, by, 1)
        return jnp.where(last, jnp.stack([turned[1], turned[0]]), turned)

    def wrap_z(pair, sign):
        by, last = (127, last_lane) if sign > 0 else (1, first_lane)
        turned = [pltpu.roll(v, by, 2) for v in pair]
        return [jnp.where(last, turned[1 - z], turned[z]) for z in range(2)]

    def odd_of(par):
        return odd if par == 0 else jnp.logical_not(odd)

    def beside_x(ref, fields, par, i, sign):
        far = min(max(i + sign, 0), 5)
        here, there = ref[fields, 1 - par, i], ref[fields, 1 - par, far]
        crosses = odd_of(par) if sign > 0 else odd_of(1 - par)
        return jnp.where(crosses, there, here)

    def features(p):
        name, sign = "f" + str(1 - p), 2 * p - 1
        for i in range(2):
            pair = 2 + i
            cells = {}
            for kind in ("d", "m"):
                fields = slice(0, 3) if kind == "d" else slice(3, 6)
                for dx in range(2):
                    for par in range(2):
                        if dx:
                            near = beside_x(flat[name], fields, par, pair, sign)
                            far = beside_x(edge[name], fields, par, pair, sign)
                        else:
                            near, far = flat[name][fields, par, pair], edge[name][fields, par, pair]
                        cells[kind, dx, par, 0] = near
                        cells[kind, dx, 1 - par, 1] = shift_z(near, far, sign)
            for par in range(2):
                own_d = flat["f" + str(p)][0:3, par, pair, 0]
                own_m = flat["f" + str(p)][3:6, par, pair, 0]
                at = (par * 2 + i) * 8
                for o in range(8):
                    dx, dy, dz = o // 4, o // 2 % 2, o % 2
                    held = (par + dy) % 2
                    near_d, near_m = cells["d", dx, held, dz], cells["m", dx, held, dz]
                    if dy:
                        near_d = shift_y(near_d[:, 0], near_d[:, 1], sign)
                        near_m = shift_y(near_m[:, 0], near_m[:, 1], sign)
                    else:
                        near_d, near_m = near_d[:, 0], near_m[:, 0]
                    diff = near_d - own_d
                    for k in range(3):
                        table[pl.ds((4 * o + k) * 32 + at, 8), :] = diff[k]
                    table[pl.ds((4 * o + 3) * 32 + at, 8), :] = jnp.sum(own_m * near_m, axis=0)

    def network(p):
        @pl.loop(0, 4, unroll=4)
        def _(chunk):
            x = jnp.concatenate(
                [table[pl.ds(chunk * 8 + r, 32, stride=32), :] for r in range(8)], axis=1
            ).astype(BF16)
            wide = jnp.concatenate([bias_wide[...]] * 8, axis=1)
            h = jnp.dot(w1[...], x, preferred_element_type=F32) + wide
            h = (h + h * jnp.tanh(h)).astype(BF16)
            h = jnp.dot(w2[...], h, preferred_element_type=F32)
            h = (h + h * jnp.tanh(h)).astype(BF16)
            h = jnp.dot(w3[...], h, preferred_element_type=F32)
            for r in range(8):
                heads[pl.ds((chunk * 8 + r) * 8, 8), :] = h[0:8, 128 * r : 128 * r + 128]

        def head(k, par, i):
            return heads[pl.ds((par * 2 + i) * 64 + k, 8, stride=8), :]

        name = "c" + str(p)
        for i in range(2):
            for par in range(2):
                flat[name][0, par, 2 + i, 0] = 1.0 + 0.5 * jnp.tanh(head(3, par, i))
        send(name, flat[name])
        for i in range(2):
            for k in range(3):
                planes = by_parity(head(k, 0, i), head(k, 1, i))
                for x in range(2):
                    results[3 * p + k, 2 * i + x] = planes[x]

    arrive_f(1)
    features(0)
    network(0)
    arrive_f(0)
    features(1)
    network(1)

    def drives(p, source):
        sign = 2 * p - 1

        def body(i):
            for k in range(3):
                along = []
                for par in range(2):
                    along.append([])
                    for ref in (flat[source], edge[source]):
                        far = min(max(i + sign, 0), 5)
                        crosses = odd_of(par) if sign > 0 else odd_of(1 - par)
                        other = jnp.where(crosses, ref[k, 1 - par, far], ref[k, 1 - par, i])
                        along[par].append(ref[k, par, i] + other)
                tall = []
                for par in range(2):
                    tall.append([])
                    for z in range(2):
                        tall[par].append(along[par][z] + wrap_y(along[1 - par][z], sign))
                for par in range(2):
                    other = wrap_z(tall[1 - par], sign)
                    for z in range(2):
                        drive[z, k, par, i] = tall[par][z] + other[z]

        for i in range(6):
            body(i)

    def turn(v, b, twice):
        square = b[0] * b[0] + b[1] * b[1] + b[2] * b[2]
        z = square * (0.0025 / 64.0)
        c = 1.0 + z * (-1 / 2 + z * (1 / 24 + z * (-1 / 720 + z * (1 / 40320 - z / 3628800))))
        s = 0.05 + z * (-0.05 / 6 + z * (0.05 / 120 + z * (-0.05 / 5040 + z * (0.05 / 362880))))
        for _ in range(3):
            s = s * c
            c = 2.0 * (c * c) - 1.0
        if twice:
            s = 2.0 * (s * c)
            c = 2.0 * (c * c) - 1.0
        q = [s * b[k] for k in range(3)]
        w = [v[k] + v[k] for k in range(3)]
        t = [q[1] * w[2] - q[2] * w[1], q[2] * w[0] - q[0] * w[2], q[0] * w[1] - q[1] * w[0]]
        r = [q[1] * t[2] - q[2] * t[1], q[2] * t[0] - q[0] * t[2], q[0] * t[1] - q[1] * t[0]]
        return [v[k] + (c * t[k] + r[k]) for k in range(3)]

    def step(p, name, sector, extent, twice=False):
        par, bit = sector % 2, float(sector // 2 % 2)
        lo, hi = {3: (0, 6), 2: (1, 5), 1: (1, 5), 0: (2, 4)}[extent]
        refs = (flat[name], edge[name])
        opened = odd_of(par)
        fields = (flat["c" + str(p)], edge["c" + str(p)])
        for i in range(lo, hi):
            inner = [[ref[k, 1 - par, i] for ref in refs] for k in range(3)]
            field = []
            for k in range(3):
                field.append([])
                up, down = wrap_z(inner[k], 1), wrap_z(inner[k], -1)
                for z in range(1 if extent == 0 else 2):
                    o = inner[k][z]
                    back = refs[z][k, 1 - par, max(i - 1, 0)]
                    ahead = refs[z][k, 1 - par, min(i + 1, 5)]
                    total = o + jnp.where(opened, ahead, back)
                    total = total + (wrap_y(o, 1) + wrap_y(o, -1)) + (up[z] + down[z])
                    field[k].append(0.5 * total + fields[z][0, par, i] * drive[z, k, par, i])
            own = [refs[0][k, par, i] for k in range(3)]
            b = [field[k][0] for k in range(3)]
            chosen = fields[0][1, par, i] == bit
            if extent == 0:
                own, b, chosen = [v[0] for v in own], [v[0] for v in b], chosen[0]
            new = turn(own, b, twice)
            for k in range(3):
                value = jnp.where(chosen, new[k], own[k])
                if extent == 0:
                    refs[0][k, par, i, 0] = value
                else:
                    refs[0][k, par, i] = value
            if extent:
                parts = [field[k][1] for k in range(3)] + [refs[1][k, par, i] for k in range(3)]
                parts.append(fields[1][1, par, i])
                if i == lo:
                    packed = parts
                else:
                    here = (lane + 4) // 8 % 16 == i - lo
                    packed = [
                        jnp.where(here, pltpu.roll(v, 8 * (i - lo), 2), t)
                        for v, t in zip(parts, packed)
                    ]
        if extent:
            new = turn(packed[3:6], packed[:3], twice)
            for k in range(3):
                value = jnp.where(packed[6] == bit, new[k], packed[3 + k])
                for i in range(lo, hi):
                    back = (128 - 8 * (i - lo)) % 128
                    refs[1][k, par, i] = pltpu.roll(value, back, 2) if back else value

    def pass_on(name, source):
        send(name, flat[source])
        flat[name][:, :, 2:4, 0] = flat[source][:, :, 2:4, 0]

    arrive("m1")
    drives(0, "m1")
    arrive("m0")
    arrive("c0")
    for k, sector in enumerate((0, 1, 2, 3)):
        step(0, "m0", sector, 3 - k)
    pass_on("e1", "m0")
    arrive("c1")
    for p in range(2):
        for c in copies_f(p):
            c.wait_send()
    for name in ("m1", "m0", "c0", "c1"):
        sent(name)
    arrive("e1")
    drives(1, "e1")
    for k, sector in enumerate((4, 5, 6, 7)):
        step(1, "m1", sector, 3 - k, sector == 7)
    pass_on("e2", "m1")
    sent("e1")
    arrive("e2")
    for k, sector in enumerate((6, 5, 4)):
        step(1, "e2", sector, 2 - k)
    pass_on("e3", "e2")
    sent("e2")
    arrive("e3")
    drives(0, "e3")
    for k, sector in enumerate((3, 2, 1, 0)):
        step(0, "e1", sector, 3 - k)
    for p, name in ((0, "e1"), (1, "e2")):
        for k in range(3):
            for i in range(2):
                planes = by_parity(flat[name][k, 0, 2 + i, 0], flat[name][k, 1, 2 + i, 0])
                for x in range(2):
                    results[6 + 3 * p + k, 2 * i + x] = planes[x]

    sent("e3")


def on_device(displacement, velocity, moments, sector_bit, weight_in, bias_in, weight_mid, weight_out):
    given = (
        displacement, moments, sector_bit,
        weight_in, bias_in, weight_mid, weight_out.T,
    )
    vmem = pl.BlockSpec(memory_space=pltpu.VMEM)
    shape = jax.ShapeDtypeStruct(displacement.shape, F32)
    count = len(NAMES)
    groups = [pltpu.VMEM((f, 2, 6, 2, 8, 128), F32) for f in GROUPS.values()]
    results = pl.pallas_call(
        kernel,
        out_shape=jax.ShapeDtypeStruct((12,) + displacement.shape[1:], F32),
        in_specs=[pl.BlockSpec(memory_space=pltpu.HBM)] * 7,
        out_specs=vmem,
        scratch_shapes=groups
        + groups
        + [
            pltpu.VMEM((count, 8, 128), F32),
            pltpu.VMEM((count, 3, 2, 2, 8, 128), F32),
            pltpu.VMEM((2, 2, 8, 128), F32),
            pltpu.VMEM((2, 3, 2, 2, 8, 128), F32),
            pltpu.VMEM((2, 3, 2, 6, 2, 8, 128), F32),
            pltpu.VMEM((1024, 128), F32),
            pltpu.VMEM((256, 128), F32),
            pltpu.VMEM((256, 32), BF16),
            pltpu.VMEM((256, 256), BF16),
            pltpu.VMEM((16, 256), BF16),
            pltpu.VMEM((256, 128), F32),
        ]
        + [pltpu.VMEM(a.shape, a.dtype) for a in given]
        + [
            pltpu.SemaphoreType.DMA((len(given),)),
            pltpu.SemaphoreType.DMA((count, 2)),
            pltpu.SemaphoreType.DMA((count, 2)),
            pltpu.SemaphoreType.DMA((2, len(UP))),
            pltpu.SemaphoreType.DMA((2, len(UP))),
        ],
        compiler_params=pltpu.CompilerParams(
            collective_id=0, has_side_effects=True, vmem_limit_bytes=60 * 1024 * 1024
        ),
    )(*given)
    velocity_out = velocity + 0.25 * results[:6]
    return displacement + 0.25 * velocity_out, velocity_out, results[6:]


def solution(mesh):
    cells = P(None, "gx", "gy", "gz")
    return jax.shard_map(
        on_device,
        mesh=mesh,
        in_specs=(cells, cells, cells, cells, P(), P(), P(), P()),
        out_specs=(cells, cells, cells),
        check_vma=False,
    )
```
